32 devices in a mesh: dp: 4 (over x, core), ctx: 8 (over z, y).
Axes of the slice: x: 2, y: 2, z: 4, core: 2. Of those that a mesh axis runs over, the one named last changes fastest.
Arguments:
- inputs: bfloat16 [32, 1024, 768], P('dp', 'ctx'), may hold values from -6 to 6
- segments: int32 [32, 1024], P('dp'), may hold values from 0 to 5, as said below
- random_blocks: int32 [32, 16, 12, 3], P('dp', 'ctx'), may hold values from 0 to 15, as said below
- cotangent: bfloat16 [32, 1024, 768], P('dp', 'ctx'), may hold values from -6 to 6
- qkv_weight: bfloat16 [768, 2304], P('dp'), may hold values from -0.21875 to 0.21875
- qv_bias: bfloat16 [1536], P('dp'), may hold values from -2 to 2
- out_weight: bfloat16 [768, 768], P('dp'), may hold values from -3.5 to 3.5
- out_bias: bfloat16 [768], P('dp'), may hold values from -2 to 2
- norm1_gain: bfloat16 [768], P('dp'), may hold values from 0.5 to 1.5
- norm1_bias: bfloat16 [768], P('dp'), may hold values from -2 to 2
- up_weight: bfloat16 [768, 3072], P('dp'), may hold values from -0.21875 to 0.21875
- up_bias: bfloat16 [3072], P('dp'), may hold values from -2 to 2
- down_weight: bfloat16 [3072, 768], P('dp'), may hold values from -0.109375 to 0.109375
- down_bias: bfloat16 [768], P('dp'), may hold values from -2 to 2
- norm2_gain: bfloat16 [768], P('dp'), may hold values from 0.5 to 1.5
- norm2_bias: bfloat16 [768], P('dp'), may hold values from -2 to 2
Outputs:
- layer_out: bfloat16 [32, 1024, 768], P('dp', 'ctx')
- input_grad: bfloat16 [32, 1024, 768], P('dp', 'ctx')
- grad_qkv_weight: float32 [768, 2304], P('dp')
- grad_qv_bias: float32 [1536], P('dp')
- grad_out_weight: float32 [768, 768], P('dp')
- grad_out_bias: float32 [768], P('dp')
- grad_norm1_gain: float32 [768], P('dp')
- grad_norm1_bias: float32 [768], P('dp')
- grad_up_weight: float32 [768, 3072], P('dp')
- grad_up_bias: float32 [3072], P('dp')
- grad_down_weight: float32 [3072, 768], P('dp')
- grad_down_bias: float32 [768], P('dp')
- grad_norm2_gain: float32 [768], P('dp')
- grad_norm2_bias: float32 [768], P('dp')
The draws below stay inside these ranges and needn't reach their ends.
Inputs may be any that keep to these rules, and one draw needn't show every extreme that they name: `segments`: segment numbers start at 0 and never fall along a sequence. In each group of 8 sequences that share an index of dp, one sequence is a single document and another packs documents of exactly 200 tokens; the others pack documents of 200 to 2000 tokens; in every packed sequence the last document is cut by the sequence's end. `random_blocks`: for each group of 8 sequences that share an index of dp and each aligned run of 2 query blocks, the entries over those sequences, blocks, heads and slots name blocks of every aligned run of 2 key blocks exactly 72 times.
All inputs are finite; a program needn't handle non-finite values.
Results may differ from the reference program's by a relative error of at most 0.015.
Values may be sent and summed in bfloat16 or wider, within the bound.
No kernel may reach another device: no remote copies, remote signals or barrier semaphores. Data moves between devices by JAX's collectives and lax.ppermute only.
A program may use at most 576 MiB of HBM per device.

```python
import jax
import jax.numpy as jnp
from jax import lax

D = 768
H = 12
HD = 64
FF = 3072
BLOCK = 64
RAND = 3
SEQ_GRP = 8
BLK_DEV = 2
DOC_MIN = 200
DOC_MAX = 2000
LEN = 1024
NBLK = 16
NSEQ = 32


def draw_segments(key, part):
    key = jax.random.fold_in(key, 11)
    doc_slots = LEN // DOC_MIN + 1
    lengths = jax.random.randint(jax.random.fold_in(key, 1), (NSEQ, doc_slots), DOC_MIN, DOC_MAX + 1)
    group_total = NSEQ // SEQ_GRP
    chosen = jax.random.randint(jax.random.fold_in(key, 2), (group_total,), 0, SEQ_GRP)
    rows_in_group = jnp.arange(NSEQ, dtype=jnp.int32) % SEQ_GRP
    single = rows_in_group == jnp.repeat(chosen, SEQ_GRP)
    shortest = rows_in_group == jnp.repeat((chosen + 1) % SEQ_GRP, SEQ_GRP)
    lengths = jnp.where(shortest[:, None], DOC_MIN, lengths)
    ends = jnp.cumsum(lengths, axis=1)
    places = jnp.arange(LEN, dtype=jnp.int32)
    numbers = jnp.sum((ends[:, None, :] <= places[None, :, None]).astype(jnp.int32), axis=2)
    return jnp.where(single[:, None], 0, numbers).astype(jnp.int32)


def draw_random_blocks(key, part):
    key = jax.random.fold_in(key, 23)
    owner_total = NBLK // BLK_DEV
    request_total = SEQ_GRP * BLK_DEV * H * RAND
    per_owner = request_total // owner_total
    group_total = NSEQ // SEQ_GRP

    def one_device(index):
        device_key = jax.random.fold_in(key, index)
        owners = jax.random.permutation(jax.random.fold_in(device_key, 1), jnp.repeat(jnp.arange(owner_total, dtype=jnp.int32), per_owner))
        within = jax.random.randint(jax.random.fold_in(device_key, 2), (request_total,), 0, BLK_DEV)
        return (owners * BLK_DEV + within).reshape(SEQ_GRP, BLK_DEV, H, RAND)
    lists = jax.vmap(one_device)(jnp.arange(group_total * owner_total))
    lists = lists.reshape(group_total, owner_total, SEQ_GRP, BLK_DEV, H, RAND)
    lists = lists.transpose(0, 2, 1, 3, 4, 5).reshape(NSEQ, NBLK, H, RAND)
    return lists.astype(jnp.int32)


def levels(stream_key, extent, shards, least, largest):
    def one(dim, shards_of):
        draws = jax.random.uniform(jax.random.fold_in(jax.random.fold_in(stream_key, 6), dim), (shards_of,), jnp.float32, least / len(shards), largest / len(shards))
        return jnp.repeat(jnp.exp(draws), extent[dim] // shards_of).reshape((-1,) + (1,) * (len(extent) - dim - 1))

    loudness = one(*shards[0])
    for cut in shards[1:]:
        loudness = loudness * one(*cut)
    return loudness


def bell_draw(rng, extent, deviation, bound, shards=(), held_as=jnp.bfloat16):
    drawn = jax.random.normal(rng, extent, jnp.float32) * deviation
    if len(shards) > 0:
        drawn = levels(rng, extent, shards, -0.22, 0.18) * drawn
    return jnp.clip(drawn, min=-bound, max=bound).astype(held_as)


def setup_inputs(seed: int = 0) -> dict:
    splits = jax.random.split(jax.random.key(seed), 17)
    inputs = bell_draw(splits[0], (NSEQ, LEN, D), 1.0, 6.0, ((0, 4), (1, 8)))
    segments = draw_segments(jax.random.fold_in(splits[16], 71), 0)
    random_blocks = draw_random_blocks(jax.random.fold_in(splits[16], 71), 0)
    cotangent = bell_draw(splits[3], (NSEQ, LEN, D), 1.0, 6.0, ((0, 4), (1, 8)))
    qkv_weight = bell_draw(splits[4], (D, 3 * D), D ** -0.5, 0.21875, ((0, 4),))
    qv_bias = bell_draw(splits[5], (2 * D,), 0.3, 2.0, ((0, 4),))
    out_weight = bell_draw(splits[6], (D, D), (max(D // 256, 1)) ** -0.5, 3.5, ((0, 4),))
    out_bias = bell_draw(splits[7], (D,), 0.3, 2.0, ((0, 4),))
    norm1_gain = jnp.clip(1.0 + 0.1 * jax.random.normal(splits[8], (D,), jnp.float32), 0.5, 1.5).astype(jnp.bfloat16)
    norm1_bias = bell_draw(splits[9], (D,), 0.3, 2.0, ((0, 4),))
    up_weight = bell_draw(splits[10], (D, FF), D ** -0.5, 0.21875, ((0, 4),))
    up_bias = bell_draw(splits[11], (FF,), 0.3, 2.0, ((0, 4),))
    down_weight = bell_draw(splits[12], (FF, D), FF ** -0.5, 0.109375, ((0, 4),))
    down_bias = bell_draw(splits[13], (D,), 0.3, 2.0, ((0, 4),))
    norm2_gain = jnp.clip(1.0 + 0.1 * jax.random.normal(splits[14], (D,), jnp.float32), 0.5, 1.5).astype(jnp.bfloat16)
    norm2_bias = bell_draw(splits[15], (D,), 0.3, 2.0, ((0, 4),))
    return {"inputs": inputs, "segments": segments, "random_blocks": random_blocks, "cotangent": cotangent, "qkv_weight": qkv_weight, "qv_bias": qv_bias, "out_weight": out_weight, "out_bias": out_bias, "norm1_gain": norm1_gain, "norm1_bias": norm1_bias, "up_weight": up_weight, "up_bias": up_bias, "down_weight": down_weight, "down_bias": down_bias, "norm2_gain": norm2_gain, "norm2_bias": norm2_bias}


@jax.custom_vjp
def low(v):
    return lax.optimization_barrier(v.astype(jnp.bfloat16)).astype(jnp.float32)

@jax.custom_vjp
def low_back(v):
    return v

def low_keep(v):
    return (low(v), None)

def low_pass(kept, grad):
    return (grad,)

def back_keep(v):
    return (v, None)

def back_low(kept, grad):
    return (low(grad),)
low.defvjp(low_keep, low_pass)
low_back.defvjp(back_keep, back_low)
precise = lax.Precision.HIGHEST
eps_norm = 1e-12
masked_score = -1e+30

def product(left, right):
    return jnp.dot(left, right, precision=precise, preferred_element_type=jnp.float32)

def layer_norm(values_in, gain_vec, offset_vec):
    centred = values_in - lax.optimization_barrier(jnp.mean(values_in, axis=-1, keepdims=True))
    variance = lax.optimization_barrier(jnp.mean(centred * centred, axis=-1, keepdims=True))
    return centred * lax.rsqrt(variance + eps_norm) * gain_vec + offset_vec

def key_lists(rand_seq):
    own_block = jnp.arange(NBLK, dtype=jnp.int32)
    fixed_lists = jnp.stack([own_block - 1, own_block, own_block + 1, own_block * 0, own_block * 0 + NBLK - 1], axis=1)
    fixed_lists = jnp.broadcast_to(fixed_lists[:, None, :], (NBLK, H, 5))
    return jnp.concatenate([fixed_lists, rand_seq.astype(jnp.int32)], axis=2)

def attend_group(queries, key_index, query_seg, key_heads, value_heads, seg_blocks):
    present = (key_index >= 0) & (key_index < NBLK)
    clipped = jnp.clip(key_index, 0, NBLK - 1)
    head_grid = jnp.arange(H, dtype=jnp.int32)[None, :, None]
    key_part = key_heads[clipped, head_grid]
    val_part = value_heads[clipped, head_grid]
    key_seg = seg_blocks[clipped]
    scores = jnp.einsum('gqhd,ghkjd->ghqkj', queries, key_part, precision=precise) * HD ** (-0.5)
    scores = low_back(scores)
    allowed = present[:, :, None, :, None] & (key_seg[:, :, None, :, :] == query_seg[:, None, :, None, None])
    scores = jnp.where(allowed, scores, masked_score)
    group_len = queries.shape[0]
    softmax_w = low(jax.nn.softmax(scores.reshape(group_len, H, BLOCK, -1), axis=-1))
    return jnp.einsum('ghqn,ghnd->gqhd', softmax_w, val_part.reshape(group_len, H, -1, HD), precision=precise)

def global_rows(query_rows, keys_in, values_in, seg_seq, row_seg):
    query_heads = query_rows.reshape(2 * BLOCK, H, HD)
    key_heads = keys_in.reshape(LEN, H, HD)
    value_heads = values_in.reshape(LEN, H, HD)
    scores = jnp.einsum('qhd,khd->hqk', query_heads, key_heads, precision=precise) * HD ** (-0.5)
    scores = low_back(scores)
    allowed = row_seg[None, :, None] == seg_seq[None, None, :]
    scores = jnp.where(allowed, scores, masked_score)
    softmax_w = low(jax.nn.softmax(scores, axis=-1))
    return jnp.einsum('hqk,khd->qhd', softmax_w, value_heads, precision=precise).reshape(2 * BLOCK, D)

def attention(queries, keys_in, values_in, seg_seq, rand_seq):
    query_blocks = queries.reshape(NBLK, BLOCK, H, HD)
    key_heads = keys_in.reshape(NBLK, BLOCK, H, HD).transpose(0, 2, 1, 3)
    value_heads = values_in.reshape(NBLK, BLOCK, H, HD).transpose(0, 2, 1, 3)
    seg_blocks = seg_seq.reshape(NBLK, BLOCK)
    key_index = key_lists(rand_seq)
    group_count = NBLK // 8

    def one_group(members):
        return attend_group(members[0], members[1], members[2], key_heads, value_heads, seg_blocks)
    sparse = lax.map(jax.checkpoint(one_group), (query_blocks.reshape(group_count, 8, BLOCK, H, HD), key_index.reshape(group_count, 8, H, -1), seg_blocks.reshape(group_count, 8, BLOCK)))
    sparse = sparse.reshape(LEN, D)
    query_rows = jnp.concatenate([queries[:BLOCK], queries[LEN - BLOCK:]], axis=0)
    row_seg = jnp.concatenate([seg_seq[:BLOCK], seg_seq[LEN - BLOCK:]], axis=0)
    whole = jax.checkpoint(global_rows)(query_rows, keys_in, values_in, seg_seq, row_seg)
    return jnp.concatenate([whole[:BLOCK], sparse[BLOCK:LEN - BLOCK], whole[BLOCK:]], axis=0)

def layer(tokens_in, seg_seq, rand_seq, params):
    weight_qkv, bias_qv, weight_out, bias_out, gain_one, shift_one, weight_up, bias_up, weight_down, bias_down, gain_two, shift_two = params
    projected = product(tokens_in, weight_qkv)
    queries = low(low_back(projected[:, :D] + bias_qv[:D]))
    keys_in = low(low_back(projected[:, D:2 * D]))
    values_in = low(low_back(projected[:, 2 * D:] + bias_qv[D:]))
    attended = low(low_back(attention(queries, keys_in, values_in, seg_seq, rand_seq)))
    branch = low_back(product(attended, weight_out) + bias_out)
    hidden = layer_norm(tokens_in + branch, gain_one, shift_one)
    up_proj = low_back(product(low(hidden), weight_up) + bias_up)
    active = low(jax.nn.gelu(up_proj, approximate=False))
    mlp_out = low_back(product(active, weight_down) + bias_down)
    return layer_norm(hidden + mlp_out, gain_two, shift_two)

def reference(inputs, segments, random_blocks, cotangent, qkv_weight, qv_bias, out_weight, out_bias, norm1_gain, norm1_bias, up_weight, up_bias, down_weight, down_bias, norm2_gain, norm2_bias):
    params = tuple((weight.astype(jnp.float32) for weight in (qkv_weight, qv_bias, out_weight, out_bias, norm1_gain, norm1_bias, up_weight, up_bias, down_weight, down_bias, norm2_gain, norm2_bias)))

    def one_sequence(totals, members):
        tokens_in, seg_seq, rand_seq, grad_seq = members

        def forward(tokens_f, weights_f):
            return layer(tokens_f, seg_seq, rand_seq, weights_f)
        result, pullback = jax.vjp(forward, tokens_in.astype(jnp.float32), params)
        token_grad, param_grads = pullback(grad_seq.astype(jnp.float32))
        totals = jax.tree.map(jnp.add, totals, param_grads)
        return (totals, (result.astype(jnp.bfloat16), token_grad.astype(jnp.bfloat16)))
    starting = tuple((jnp.zeros_like(weight) for weight in params))
    totals, (layer_out, input_grad) = lax.scan(one_sequence, starting, (inputs, segments, random_blocks, cotangent))
    return (layer_out, input_grad, totals[0], totals[1], totals[2], totals[3], totals[4], totals[5], totals[6], totals[7], totals[8], totals[9], totals[10], totals[11])
```

```python
import jax
import jax.numpy as jnp
from jax import lax
from jax.experimental import pallas as pl
from jax.experimental.pallas import tpu as pltpu
from jax.sharding import PartitionSpec as P

f32, bf16 = jnp.float32, jnp.bfloat16
eps_norm = 1e-12
far = 1e30
doc_min = 200
lanes_n = 128
vmem_cap = 56 * 2**20


def swap_pieces(pieces, axis, stride):
    count, size = pieces.shape[0], lax.axis_size(axis)
    groups = None
    if count < size:
        span = stride * count
        starts = [base + offset for base in range(0, size, span) for offset in range(stride)]
        groups = [[start + i * stride for i in range(count)] for start in starts]
    return lax.all_to_all(pieces, axis, 0, 0, axis_index_groups=groups, tiled=True)


def share_pieces(piece, axis, stride, count):
    size = lax.axis_size(axis)
    member = (lax.axis_index(axis) // stride) % count
    came = [piece]
    for k in range(1, count):
        pairs = [(i, ((i // stride % count) ^ k) * stride + i % stride + i // (stride * count) * (stride * count)) for i in range(size)]
        came.append(lax.ppermute(piece, axis, pairs))
    came = jnp.stack(came)
    return jnp.stack([lax.dynamic_index_in_dim(came, member ^ i, 0, keepdims=False) for i in range(count)])


def sum_pieces(pieces, axis, stride):
    count = pieces.shape[0]
    size = lax.axis_size(axis)
    member = (lax.axis_index(axis) // stride) % count
    total = lax.dynamic_index_in_dim(pieces, member, 0, keepdims=False).astype(f32)
    for k in range(1, count):
        pairs = [(i, ((i // stride % count) ^ k) * stride + i % stride + i // (stride * count) * (stride * count)) for i in range(size)]
        out = lax.dynamic_index_in_dim(pieces, member ^ k, 0, keepdims=False)
        total = total + lax.ppermute(out.astype(bf16), axis, pairs).astype(f32)
    return total


def stages_of(size):
    stages, stride = [], 1
    while stride < size:
        count = 2 if stride == 1 else min(4, size // stride)
        stages.append((stride, count))
        stride *= count
    return stages


def cut(value, dim, count):
    rows, cols = value.shape
    if dim == 0:
        return value.reshape(count, rows // count, cols)
    return jnp.stack([value[:, i * (cols // count) : (i + 1) * (cols // count)] for i in range(count)])


def joined(pieces, dim):
    return jnp.concatenate([pieces[i] for i in range(pieces.shape[0])], axis=dim)


def reduce_dp(grad):
    count = grad.shape[0]
    total, stride = grad, 1
    while stride < count:
        half = total.reshape(total.shape[0] // 2, 2, *grad.shape[1:]).transpose(1, 0, 2, 3)
        total = sum_pieces(half, "dp", stride).astype(bf16)
        stride *= 2
    return total[0]


def reduce_ctx(grad):
    stages = stages_of(lax.axis_size("ctx"))
    total = grad
    for place, (stride, count) in enumerate(stages):
        total = sum_pieces(cut(total, (place + 1) % 2, count), "ctx", stride).astype(bf16)
    for place, (stride, count) in reversed(list(enumerate(stages))):
        total = joined(share_pieces(total, "ctx", stride, count), (place + 1) % 2)
    return total


def reduce_all(grad):
    return reduce_ctx(reduce_dp(grad))


def mask_features(seg, rand, block):
    tokens = seg.shape[0]
    blocks, heads = rand.shape[:2]
    seg_limit = tokens // doc_min + 1
    used = seg_limit + 2 * blocks
    width = -(-used // lanes_n) * lanes_n
    ids = jnp.arange(blocks, dtype=jnp.int32)

    def hot(values):
        return (values[..., None] == ids).astype(jnp.int32)

    near = hot(ids - 1) + hot(ids) + hot(ids + 1) + hot(ids * 0) + hot(ids * 0 + blocks - 1)
    counts = near[:, None, :] + jnp.sum(hot(rand), axis=2)
    edge = (ids == 0) | (ids == blocks - 1)
    counts = jnp.where(edge[:, None, None], 1, counts).transpose(1, 2, 0)
    log_count = jnp.log(jnp.maximum(counts, 1).astype(f32))
    high = log_count.astype(bf16).astype(f32)
    low = jnp.where(counts > 0, log_count - high, 0.0)
    high = jnp.where(counts > 0, high, -far)
    table = jnp.concatenate(
        [
            jnp.zeros((heads, blocks, seg_limit), f32),
            high,
            low,
            jnp.zeros((heads, blocks, width - used), f32),
        ],
        axis=2,
    )
    lane = jnp.arange(width, dtype=jnp.int32)[None]
    own = (jnp.arange(tokens, dtype=jnp.int32) // block)[:, None]
    is_seg = lane < seg_limit
    same = lane == seg[:, None]
    key_feat = jnp.where(is_seg & same, 1.0, 0.0).astype(bf16)
    own_lane = (lane - seg_limit == own) | (lane - seg_limit - blocks == own)
    query_feat = jnp.where(
        is_seg, jnp.where(same, 0.0, -far), jnp.where(own_lane, 1.0, 0.0)
    ).astype(bf16)
    return key_feat, query_feat, table


def fill_keys(k_ref, key_feat_ref, table_ref, keys):
    tokens, width = key_feat_ref.shape
    blocks = table_ref.shape[1]
    feat = key_feat_ref[...].astype(f32).reshape(blocks, tokens // blocks, width) + table_ref[0][:, None, :]
    keys[:, :lanes_n] = k_ref[...]
    keys[:, lanes_n:] = feat.reshape(tokens, width).astype(bf16)


def forward_kernel(
    q_ref, k_ref, v_ref, key_feat_ref, query_feat_ref, table_ref, out_ref, keys, vals, *, half, tile
):
    side = pl.program_id(1)
    tokens = q_ref.shape[0]
    fill_keys(k_ref, key_feat_ref, table_ref, keys)
    vals[:, :lanes_n] = v_ref[...]
    vals[:, lanes_n:] = jnp.ones((tokens, lanes_n), bf16)

    @pl.loop(0, tokens // tile)
    def _(step):
        rows = pl.ds(pl.multiple_of(step * tile, tile), tile)
        keep = lax.broadcasted_iota(jnp.int32, (tile, lanes_n), 1) // half == side
        q = jnp.where(keep, q_ref[rows, :] * bf16(half**-0.5), bf16(0))
        q = jnp.concatenate([q, query_feat_ref[rows, :]], axis=1)
        scores = lax.dot_general(
            q, keys[...], (((1,), (1,)), ((), ())), preferred_element_type=f32
        )
        top = jnp.max(scores, axis=1, keepdims=True)
        weights = jnp.exp(scores - top).astype(bf16)
        mixed = jnp.dot(weights, vals[...], preferred_element_type=f32)
        out = (mixed[:, :lanes_n] / mixed[:, lanes_n:]).astype(bf16)
        other = jnp.where(side == 0, jnp.zeros_like(out), out_ref[rows, :])
        out_ref[rows, :] = jnp.where(keep, out, other)


def backward_kernel(
    q_ref,
    k_ref,
    v_ref,
    grad_ref,
    key_feat_ref,
    query_feat_ref,
    table_ref,
    dq_ref,
    dk_ref,
    dv_ref,
    keys,
    dk_sum,
    dv_sum,
    *,
    half,
    tile,
):
    side = pl.program_id(1)
    tokens = q_ref.shape[0]
    fill_keys(k_ref, key_feat_ref, table_ref, keys)

    @pl.when(side == 0)
    def _():
        dk_sum[...] = jnp.zeros_like(dk_sum)
        dv_sum[...] = jnp.zeros_like(dv_sum)
        dq_ref[...] = jnp.zeros_like(dq_ref)

    @pl.loop(0, tokens // tile)
    def _(step):
        rows = pl.ds(pl.multiple_of(step * tile, tile), tile)
        keep = lax.broadcasted_iota(jnp.int32, (tile, lanes_n), 1) // half == side
        q = jnp.where(keep, q_ref[rows, :] * bf16(half**-0.5), bf16(0))
        grad = jnp.where(keep, grad_ref[rows, :], bf16(0))
        q_wide = jnp.concatenate([q, query_feat_ref[rows, :]], axis=1)
        scores = lax.dot_general(
            keys[...], q_wide, (((1,), (1,)), ((), ())), preferred_element_type=f32
        )
        raw = jnp.exp(scores - jnp.max(scores, axis=0, keepdims=True))
        probs = raw * (1.0 / jnp.sum(raw, axis=0, keepdims=True))
        dprobs = lax.dot_general(
            v_ref[...], grad, (((1,), (1,)), ((), ())), preferred_element_type=f32
        )
        inner = jnp.sum(probs * dprobs, axis=0, keepdims=True)
        dscores = (probs * (dprobs - inner)).astype(bf16)
        dv_sum[...] += jnp.dot(probs.astype(bf16), grad, preferred_element_type=f32)
        dk_sum[...] += jnp.dot(dscores, q, preferred_element_type=f32)
        dq = lax.dot_general(
            dscores, k_ref[...], (((0,), (0,)), ((), ())), preferred_element_type=f32
        )
        dq_ref[rows, :] += jnp.where(keep, (dq * half**-0.5).astype(bf16), bf16(0))

    @pl.when(side == 1)
    def _():
        dk_ref[...] = dk_sum[...].astype(bf16)
        dv_ref[...] = dv_sum[...].astype(bf16)


def attend(kernel, arrays, features, outs, scratch_n, half, name, after=(), first=0, count=None):
    tokens, width = arrays[0].shape
    key_feat, query_feat, table = features
    count = width // lanes_n if count is None else count
    feat_width = key_feat.shape[1]
    tile = 256 if tokens <= 2048 else 128
    pair = pl.BlockSpec((tokens, lanes_n), lambda p, s: (0, p + first))
    pair_out = pl.BlockSpec((tokens, lanes_n), lambda p, s: (0, p))
    whole = pl.BlockSpec((tokens, feat_width), lambda p, s: (0, 0), pipeline_mode=pl.Buffered(1))
    shape = jax.ShapeDtypeStruct((tokens, count * lanes_n), bf16)
    scratch = [pltpu.VMEM((tokens, lanes_n + feat_width), bf16)]
    if scratch_n == 1:
        scratch = scratch + [pltpu.VMEM((tokens, 2 * lanes_n), bf16)]
    else:
        scratch = scratch + [pltpu.VMEM((tokens, lanes_n), f32)] * 2
    work = count * lanes_n // half * tokens * tokens

    def run(*refs):
        held = len(arrays) + 3
        kernel(*refs[:held], *refs[held + len(after) :], half=half, tile=tile)

    return pl.pallas_call(
        run,
        grid=(count, 2),
        in_specs=[pair] * len(arrays)
        + [whole, whole]
        + [pl.BlockSpec((1,) + table.shape[1:], lambda p, s: (2 * (p + first) + s, 0, 0))]
        + [pl.BlockSpec(memory_space=pl.ANY)] * len(after),
        out_specs=[pair_out] * outs,
        out_shape=[shape] * outs,
        scratch_shapes=scratch,
        compiler_params=pltpu.CompilerParams(vmem_limit_bytes=vmem_cap),
        cost_estimate=pl.CostEstimate(
            flops=work * 1024 * (1 if outs == 1 else 2),
            bytes_accessed=tokens * width * 2 * (len(arrays) + outs),
            transcendentals=work,
        ),
        name=name,
    )(*arrays, key_feat, query_feat, table, *after)


def pack_kernel(weight_ref, *refs):
    out_ref = refs[-1]
    rows = weight_ref.shape[0]
    out_ref[:rows, :] = weight_ref[...]
    out_ref[rows:, :] = jnp.zeros_like(out_ref[rows:, :])
    for place, ref in enumerate(refs[:-1]):
        out_ref[rows + place : rows + place + 1, : ref.shape[1]] = ref[...]


def pack_weights(weight, vectors):
    rows, cols = weight.shape
    extra = -(-len(vectors) // 16) * 16
    return pl.pallas_call(
        pack_kernel,
        out_shape=jax.ShapeDtypeStruct((rows + extra, cols), weight.dtype),
        name="pack_weights",
    )(weight, *[v[None] for v in vectors])


def norm_forward(values_in, gain_vec, offset_vec):
    centred = values_in - jnp.mean(values_in, axis=-1, keepdims=True)
    inverse = lax.rsqrt(jnp.mean(centred * centred, axis=-1, keepdims=True) + eps_norm)
    normed = centred * inverse
    return (normed * gain_vec + offset_vec, normed, inverse)


def norm_backward(incoming, normed, inverse, gain_vec):
    scaled = incoming * gain_vec
    centred_grad = (
        scaled
        - jnp.mean(scaled, axis=-1, keepdims=True)
        - normed * jnp.mean(scaled * normed, axis=-1, keepdims=True)
    )
    return (centred_grad * inverse, jnp.sum(incoming * normed, axis=0), jnp.sum(incoming, axis=0))


def body(
    inputs,
    segments,
    random_blocks,
    cotangent,
    qkv_weight,
    qv_bias,
    out_weight,
    out_bias,
    norm1_gain,
    norm1_bias,
    up_weight,
    up_bias,
    down_weight,
    down_bias,
    norm2_gain,
    norm2_bias,
):
    seq_count, run, width = inputs.shape
    per_dev, head_count, rand_count = random_blocks.shape[1:]
    block = run // per_dev
    head_size = width // head_count
    dp_count = lax.axis_size("dp")
    ctx_count = lax.axis_size("ctx")
    ctx_index = lax.axis_index("ctx")
    team = ctx_count // seq_count
    tokens = seq_count * run

    x = swap_pieces(inputs, "ctx", team).reshape(tokens, width)
    lists = swap_pieces(random_blocks.reshape(seq_count, 1, -1), "ctx", team)
    grad_result = swap_pieces(cotangent, "ctx", team).reshape(tokens, width)

    def back_to_runs(rows):
        return swap_pieces(rows.reshape(seq_count, run, width), "ctx", team)

    vectors = (qv_bias, out_bias, norm1_gain, norm1_bias, up_bias, down_bias, norm2_gain, norm2_bias)
    sizes = [v.shape[0] for v in vectors]
    qkv_rows, qkv_cols = qkv_weight.shape
    first = lax.all_gather(pack_weights(qkv_weight, vectors), "dp", axis=0)
    weight_qkv = first[:, :qkv_rows].reshape(-1, qkv_cols)
    split = [
        first[:, qkv_rows + place, :size].reshape(-1).astype(f32) for place, size in enumerate(sizes)
    ]
    bias_qv, bias_out, gain_one, shift_one, bias_up, bias_down, gain_two, shift_two = split
    weight_out = lax.all_gather(out_weight, "dp", axis=0, tiled=True)
    weight_up = lax.all_gather(up_weight, "dp", axis=0, tiled=True)
    weight_down = lax.all_gather(down_weight, "dp", axis=0, tiled=True)

    seq_index = ctx_index // team
    seg = lax.dynamic_index_in_dim(segments, seq_index, 0, keepdims=False)
    lists = lists.reshape(seq_count, per_dev, head_count, rand_count)
    if team > 1:
        team_index = ctx_index % team
        held = -(-head_count // (2 * team)) * 2
        spare = held * team - head_count
        lists = share_pieces(lists, "ctx", 1, team).transpose(1, 0, 2, 3, 4)
        lists = jnp.pad(lists.reshape(-1, head_count, rand_count), ((0, 0), (0, spare), (0, 0)))
        lists = lax.dynamic_slice_in_dim(lists, team_index * held, held, 1)
    else:
        lists = lists.reshape(-1, head_count, rand_count)
    features = mask_features(seg, lists, block)

    def to_heads(rows):
        if team == 1:
            return rows
        rows = jnp.pad(rows, ((0, 0), (0, spare * head_size)))
        part = swap_pieces(rows.reshape(tokens, team, -1).transpose(1, 0, 2), "ctx", 1)
        part = part.reshape(team, seq_count, run, -1).transpose(1, 0, 2, 3)
        return part.reshape(team * tokens, -1)

    def to_tokens(part):
        if team == 1:
            return part
        part = part.reshape(seq_count, team, run, -1).transpose(1, 0, 2, 3)
        rows = swap_pieces(part.reshape(team, tokens, -1), "ctx", 1)
        return rows.transpose(1, 0, 2).reshape(tokens, -1)[:, :width]

    projected = jnp.dot(x, weight_qkv, preferred_element_type=f32)
    queries = (projected[:, :width] + bias_qv[:width]).astype(bf16)
    keys = projected[:, width : 2 * width].astype(bf16)
    values = (projected[:, 2 * width :] + bias_qv[width:]).astype(bf16)
    heads = tuple(to_heads(part) for part in (queries, keys, values))
    attended = attend(forward_kernel, heads, features, 1, 1, head_size, "attend_forward")[0]
    attended = to_tokens(attended)
    branch = jnp.dot(attended, weight_out, preferred_element_type=f32) + bias_out
    hidden, normed_one, inverse_one = norm_forward(x.astype(f32) + branch, gain_one, shift_one)
    hidden_low = hidden.astype(bf16)
    upper = jnp.dot(hidden_low, weight_up, preferred_element_type=f32) + bias_up
    cdf = 0.5 * (1.0 + lax.erf(upper * 0.5**0.5))
    active = (upper * cdf).astype(bf16)
    slope = (cdf + upper * jnp.exp(-0.5 * upper * upper) * (2.0 * jnp.pi) ** -0.5).astype(bf16)
    mlp_out = jnp.dot(active, weight_down, preferred_element_type=f32) + bias_down
    result, normed_two, inverse_two = norm_forward(hidden + mlp_out, gain_two, shift_two)
    layer_out = back_to_runs(result.astype(bf16))

    grad_sum, grad_gain_two, grad_shift_two = norm_backward(
        grad_result.astype(f32), normed_two, inverse_two, gain_two
    )
    grad_mlp = grad_sum.astype(bf16)

    def weight_grad(left, right):
        grad = lax.dot_general(left, right, (((0,), (0,)), ((), ())), preferred_element_type=f32)
        return grad.astype(bf16).reshape(dp_count, -1, grad.shape[1])

    down_total = reduce_all(weight_grad(active, grad_mlp))
    grad_down_b = jnp.sum(grad_mlp, axis=0, dtype=f32)
    grad_active = lax.dot_general(
        grad_mlp, weight_down, (((1,), (1,)), ((), ())), preferred_element_type=f32
    )
    grad_upper = (grad_active * slope.astype(f32)).astype(bf16)
    up_total = reduce_all(weight_grad(hidden_low, grad_upper))
    grad_up_b = jnp.sum(grad_upper, axis=0, dtype=f32)
    grad_hidden = grad_sum + lax.dot_general(
        grad_upper, weight_up, (((1,), (1,)), ((), ())), preferred_element_type=f32
    )
    grad_pre, grad_gain_one, grad_shift_one = norm_backward(
        grad_hidden, normed_one, inverse_one, gain_one
    )
    grad_branch = grad_pre.astype(bf16)
    out_total = reduce_all(weight_grad(attended, grad_branch))
    grad_out_b = jnp.sum(grad_branch, axis=0, dtype=f32)
    grad_att = lax.dot_general(
        grad_branch, weight_out, (((1,), (1,)), ((), ())), preferred_element_type=f32
    ).astype(bf16)
    back = attend(
        backward_kernel, heads + (to_heads(grad_att),), features, 3, 2, head_size, "attend_backward"
    )
    grad_proj = jnp.concatenate([to_tokens(part) for part in back], axis=1)
    grad_input = grad_pre + lax.dot_general(
        grad_proj, weight_qkv, (((1,), (1,)), ((), ())), preferred_element_type=f32
    )
    input_grad = back_to_runs(grad_input.astype(bf16))
    grad_qkv_b = jnp.sum(grad_proj, axis=0, dtype=f32)
    grad_qv_b = jnp.concatenate([grad_qkv_b[:width], grad_qkv_b[2 * width :]])
    grad_vecs = (
        grad_qv_b,
        grad_out_b,
        grad_gain_one,
        grad_shift_one,
        grad_up_b,
        grad_down_b,
        grad_gain_two,
        grad_shift_two,
    )
    per_row = -(-sum(sizes) // qkv_rows)
    side = jnp.concatenate([v.astype(bf16).reshape(dp_count, -1) for v in grad_vecs], axis=1)
    side = jnp.pad(side, ((0, 0), (0, per_row * qkv_rows - sum(sizes))))
    side = side.reshape(dp_count, qkv_rows, per_row)
    side_cols = -(-per_row // (2 * lanes_n)) * 2 * lanes_n
    side = jnp.pad(side, ((0, 0), (0, 0), (0, side_cols - per_row)))
    last = jnp.concatenate([weight_grad(x, grad_proj), side], axis=2)
    last_total = reduce_all(last).astype(f32)
    qkv_total = last_total[:, :qkv_cols]
    flat_total = last_total[:, qkv_cols : qkv_cols + per_row].reshape(-1)
    vec_totals, start = [], 0
    for size in sizes:
        vec_totals.append(flat_total[start : start + size])
        start += size
    return (
        layer_out,
        input_grad,
        qkv_total,
        vec_totals[0],
        out_total.astype(f32),
        vec_totals[1],
        vec_totals[2],
        vec_totals[3],
        up_total.astype(f32),
        vec_totals[4],
        down_total.astype(f32),
        vec_totals[5],
        vec_totals[6],
        vec_totals[7],
    )


def solution(mesh):
    tokens = P("dp", "ctx", None)
    matrix, vector = P("dp", None), P("dp")
    weights = (matrix, vector, matrix, vector, vector, vector, matrix, vector, matrix, vector, vector, vector)
    return jax.shard_map(
        body,
        mesh=mesh,
        in_specs=(tokens, matrix, P("dp", "ctx", None, None), tokens) + weights,
        out_specs=(tokens, tokens) + weights,
        check_vma=False,
    )
```

```python
import functools

import jax
import jax.numpy as jnp
from jax import lax
from jax.experimental import pallas as pl
from jax.experimental.pallas import tpu as pltpu
from jax.sharding import PartitionSpec as P

f32, bf16 = jnp.float32, jnp.bfloat16
eps_norm = 1e-12
far = 1e30
doc_min = 200
lanes_n = 128
vmem_cap = 56 * 2**20


def swap_pieces(pieces, axis, stride):
    count, size = pieces.shape[0], lax.axis_size(axis)
    groups = None
    if count < size:
        span = stride * count
        starts = [base + offset for base in range(0, size, span) for offset in range(stride)]
        groups = [[start + i * stride for i in range(count)] for start in starts]
    return lax.all_to_all(pieces, axis, 0, 0, axis_index_groups=groups, tiled=True)


def partners(axis, stride, count, k):
    return [
        (i, i + (((i // stride % count) ^ k) - i // stride % count) * stride)
        for i in range(lax.axis_size(axis))
    ]


def in_order(came, member):
    bit = 1
    while bit < len(came):
        turned = (member // bit) % 2 == 1
        came = [jnp.where(turned, came[i ^ bit], came[i]) for i in range(len(came))]
        bit *= 2
    return came


def share_pieces(piece, axis, stride, count):
    member = (lax.axis_index(axis) // stride) % count
    came = [piece]
    for k in range(1, count):
        came.append(lax.ppermute(piece, axis, partners(axis, stride, count, k)))
    return in_order(came, member)


def stages_of(size):
    stages, stride = [], 1
    while stride < size:
        stages.append((stride, 2))
        stride *= 2
    return stages


def tied(value, *deps):
    def nothing(*refs):
        pass

    return pl.pallas_call(
        nothing,
        in_specs=[pl.BlockSpec(memory_space=pl.ANY)] * (1 + len(deps)),
        out_specs=pl.BlockSpec(memory_space=pl.ANY),
        out_shape=jax.ShapeDtypeStruct(value.shape, value.dtype),
        input_output_aliases={0: 0},
        name="tied",
    )(value, *deps)


class Chain:
    def __init__(self, value, axis):
        self.value, self.plan = value, []
        if axis == "dp":
            stride = 1
            while stride < lax.axis_size("dp"):
                self.plan.append(("dp", stride, 2, True))
                stride *= 2
        else:
            stages = stages_of(lax.axis_size("ctx"))
            self.plan += [("ctx", stride, count, True) for stride, count in stages]
            self.plan += [("ctx", stride, count, False) for stride, count in reversed(stages)]

    def begin(self, *after):
        axis, stride, count, adds = self.plan[0]
        member = (lax.axis_index(axis) // stride) % count
        self.pieces = None
        if adds:
            rows, cols = self.value.shape
            outer = lax.axis_size("dp") // (2 * stride) if axis == "dp" else 1
            self.pieces = self.value.reshape(outer, count, rows // (outer * count), cols)
        else:
            self.value = tied(self.value, *after)
        self.came, self.sent = [], []
        for k in range(1, count):
            piece = self.value
            if adds:
                piece = lax.dynamic_index_in_dim(self.pieces, member ^ k, 1, keepdims=False)
                piece = tied(piece, *after)
            self.sent.append(piece)
            self.came.append(lax.ppermute(piece, axis, partners(axis, stride, count, k)))
        return self.sent[-1]

    def end(self, *after):
        axis, stride, count, adds = self.plan.pop(0)
        if after:
            self.came[0] = tied(self.came[0], *after)
        member = (lax.axis_index(axis) // stride) % count
        if adds:
            total = lax.dynamic_index_in_dim(self.pieces, member, 1, keepdims=False).astype(f32)
            for piece in self.came:
                total = total + piece.astype(f32)
            self.value = total.astype(bf16).reshape(-1, self.value.shape[1])
        else:
            self.value = jnp.concatenate(in_order([self.value] + self.came, member), axis=0)
        return self.value

    def open(self):
        return len(self.plan) > 0


def scattered(grad):
    return lax.psum_scatter(grad, "dp", scatter_dimension=0, tiled=True)


def mask_features(seg, rand, block):
    tokens = seg.shape[0]
    blocks, heads = rand.shape[:2]
    seg_limit = tokens // doc_min + 1
    used = seg_limit + 2 * blocks
    width = -(-used // lanes_n) * lanes_n
    ids = jnp.arange(blocks, dtype=jnp.int32)

    def hot(values):
        return (values[..., None] == ids).astype(jnp.int32)

    near = hot(ids - 1) + hot(ids) + hot(ids + 1) + hot(ids * 0) + hot(ids * 0 + blocks - 1)
    counts = near[:, None, :] + jnp.sum(hot(rand), axis=2)
    edge = (ids == 0) | (ids == blocks - 1)
    counts = jnp.where(edge[:, None, None], 1, counts).transpose(1, 2, 0)
    log_count = jnp.log(jnp.maximum(counts, 1).astype(f32))
    high = log_count.astype(bf16).astype(f32)
    low = jnp.where(counts > 0, log_count - high, 0.0)
    high = jnp.where(counts > 0, high, -far)
    table = jnp.concatenate(
        [
            jnp.zeros((heads, blocks, seg_limit), f32),
            high,
            low,
            jnp.zeros((heads, blocks, width - used), f32),
        ],
        axis=2,
    )
    lane = jnp.arange(width, dtype=jnp.int32)[None]
    own = (jnp.arange(tokens, dtype=jnp.int32) // block)[:, None]
    is_seg = lane < seg_limit
    same = lane == seg[:, None]
    key_feat = jnp.where(is_seg & same, 1.0, 0.0).astype(bf16)
    own_lane = (lane - seg_limit == own) | (lane - seg_limit - blocks == own)
    query_feat = jnp.where(
        is_seg, jnp.where(same, 0.0, -far), jnp.where(own_lane, 1.0, 0.0)
    ).astype(bf16)
    near = -(-seg_limit // lanes_n) * lanes_n
    return key_feat[:, :near], query_feat[:, :near], table


def fill_keys(k_ref, key_feat_ref, table_ref, keys):
    tokens, near = key_feat_ref.shape
    blocks, width = table_ref.shape[1:]
    feat = key_feat_ref[...].astype(f32).reshape(blocks, tokens // blocks, near)
    for side in range(2):
        rows = table_ref[side][:, None, :]
        both = (feat + rows[..., :near]).reshape(tokens, near)
        keys[side, :, :lanes_n] = k_ref[...]
        keys[side, :, lanes_n : lanes_n + near] = both.astype(bf16)
        if width > near:
            rest = jnp.broadcast_to(rows[..., near:], (blocks, tokens // blocks, width - near))
            keys[side, :, lanes_n + near :] = rest.reshape(tokens, width - near).astype(bf16)


def query_lanes(near_feat, start, tokens, blocks, width):
    rows, near = near_feat.shape
    if width == near:
        return near_feat
    shape = (rows, width - near)
    lane = lax.broadcasted_iota(jnp.int32, shape, 1) + near - (tokens // doc_min + 1)
    own = (lax.broadcasted_iota(jnp.int32, shape, 0) + start) // (tokens // blocks)
    rest = jnp.where((lane == own) | (lane - blocks == own), 1.0, 0.0).astype(bf16)
    return jnp.concatenate([near_feat, rest], axis=1)


rows_by_rows = (((1,), (1,)), ((), ()))
cols_by_cols = (((0,), (0,)), ((), ()))


def dot(left, right, dims=(((1,), (0,)), ((), ()))):
    return lax.dot_general(left, right, dims, preferred_element_type=f32)


def forward_kernel(
    q_ref, k_ref, v_ref, key_feat_ref, query_feat_ref, table_ref, out_ref, keys, vals, *, half, tile
):
    tokens = q_ref.shape[0]
    fill_keys(k_ref, key_feat_ref, table_ref, keys)
    vals[:, :lanes_n] = v_ref[...]
    vals[:, lanes_n:] = jnp.ones((tokens, lanes_n), bf16)

    @pl.loop(0, tokens // tile)
    def _(step):
        rows = pl.ds(pl.multiple_of(step * tile, tile), tile)
        q = q_ref[rows, :] * bf16(half**-0.5)
        side_of = lax.broadcasted_iota(jnp.int32, (tile, lanes_n), 1) // half
        feat = query_lanes(query_feat_ref[rows, :], step * tile, tokens, *table_ref.shape[1:])
        scores = [
            dot(
                jnp.concatenate([jnp.where(side_of == side, q, bf16(0)), feat], axis=1),
                keys[side],
                rows_by_rows,
            )
            for side in range(2)
        ]
        outs = []
        for score in scores:
            weights = jnp.exp(score - jnp.max(score, axis=1, keepdims=True)).astype(bf16)
            mixed = dot(weights, vals[...])
            outs.append(mixed[:, :lanes_n] / mixed[:, lanes_n:])
        out_ref[rows, :] = jnp.where(side_of == 0, outs[0], outs[1]).astype(bf16)


def backward_kernel(
    q_ref,
    k_ref,
    v_ref,
    grad_ref,
    key_feat_ref,
    query_feat_ref,
    table_ref,
    dq_ref,
    dk_ref,
    dv_ref,
    sums_ref,
    keys,
    dk_sum,
    dv_sum,
    *,
    half,
    tile,
):
    tokens = q_ref.shape[0]
    fill_keys(k_ref, key_feat_ref, table_ref, keys)
    dk_sum[...] = jnp.zeros_like(dk_sum)
    dv_sum[...] = jnp.zeros_like(dv_sum)
    sums_ref[...] = jnp.zeros_like(sums_ref)

    @pl.loop(0, tokens // tile)
    def _(step):
        rows = pl.ds(pl.multiple_of(step * tile, tile), tile)
        q_pair = q_ref[rows, :] * bf16(half**-0.5)
        grad_pair = grad_ref[rows, :]
        side_of = lax.broadcasted_iota(jnp.int32, (tile, lanes_n), 1) // half
        feat = query_lanes(query_feat_ref[rows, :], step * tile, tokens, *table_ref.shape[1:])
        queries = [jnp.where(side_of == side, q_pair, bf16(0)) for side in range(2)]
        grads = [jnp.where(side_of == side, grad_pair, bf16(0)) for side in range(2)]
        probs, dscores = [], []
        for side in range(2):
            wide = jnp.concatenate([queries[side], feat], axis=1)
            scores = dot(wide, keys[side], rows_by_rows)
            dprobs = dot(grads[side], v_ref[...], rows_by_rows)
            raw = jnp.exp(scores - jnp.max(scores, axis=1, keepdims=True))
            prob = raw * (1.0 / jnp.sum(raw, axis=1, keepdims=True))
            both = prob * dprobs
            dscore = both - prob * jnp.sum(both, axis=1, keepdims=True)
            probs.append(prob.astype(bf16))
            dscores.append(dscore.astype(bf16))
        dv_sum[...] += dot(
            jnp.concatenate(probs, axis=0), jnp.concatenate(grads, axis=0), cols_by_cols
        )
        dk_sum[...] += dot(
            jnp.concatenate(dscores, axis=0), jnp.concatenate(queries, axis=0), cols_by_cols
        )
        dqs = [dot(dscore, k_ref[...]) for dscore in dscores]
        dq = (jnp.where(side_of == 0, dqs[0], dqs[1]) * half**-0.5).astype(bf16)
        dq_ref[rows, :] = dq
        sums_ref[0:1, :] += jnp.sum(dq.astype(f32), axis=0, keepdims=True)

    dk_ref[...] = dk_sum[...].astype(bf16)
    dv = dv_sum[...].astype(bf16)
    dv_ref[...] = dv
    sums_ref[1:2, :] = jnp.sum(dv.astype(f32), axis=0, keepdims=True)


def attend(kernel, arrays, features, outs, half, name, after=(), first=0, count=None):
    tokens, width = arrays[0].shape
    key_feat, query_feat, table = features
    count = width // lanes_n if count is None else count
    near, feat_width = key_feat.shape[1], table.shape[2]
    tile = tokens if tokens <= 1024 else 32
    once = {"pipeline_mode": pl.Buffered(1)} if count == 1 else {}
    pair = pl.BlockSpec((tokens, lanes_n), lambda p: (0, p + first), **once)
    pair_out = pl.BlockSpec((tokens, lanes_n), lambda p: (0, p), **once)
    whole = pl.BlockSpec((tokens, near), lambda p: (0, 0), pipeline_mode=pl.Buffered(1))
    shape = jax.ShapeDtypeStruct((tokens, count * lanes_n), bf16)
    scratch = [pltpu.VMEM((2, tokens, lanes_n + feat_width), bf16)]
    if outs == 1:
        scratch = scratch + [pltpu.VMEM((tokens, 2 * lanes_n), bf16)]
    else:
        scratch = scratch + [pltpu.VMEM((tokens, lanes_n), f32)] * 2

    def run(*refs):
        held = len(arrays) + 3
        kernel(*refs[:held], *refs[held + len(after) :], half=half, tile=tile)

    return pl.pallas_call(
        run,
        grid=(count,),
        in_specs=[pair] * len(arrays)
        + [whole, whole]
        + [pl.BlockSpec((2,) + table.shape[1:], lambda p: (p + first, 0, 0))]
        + [pl.BlockSpec(memory_space=pl.ANY)] * len(after),
        out_specs=[pair_out] * outs + [pl.BlockSpec((8, lanes_n), lambda p: (0, p))] * (outs > 1),
        out_shape=[shape] * outs
        + [jax.ShapeDtypeStruct((8, count * lanes_n), f32)] * (outs > 1),
        scratch_shapes=scratch,
        compiler_params=pltpu.CompilerParams(vmem_limit_bytes=vmem_cap),
        cost_estimate=pl.CostEstimate(flops=0, bytes_accessed=tokens, transcendentals=0),
        name=name,
    )(*arrays, key_feat, query_feat, table, *after)


def pack_kernel(weight_ref, *refs):
    out_ref = refs[-1]
    rows = weight_ref.shape[0]
    out_ref[:rows, :] = weight_ref[...]
    out_ref[rows:, :] = jnp.zeros_like(out_ref[rows:, :])
    for place, ref in enumerate(refs[:-1]):
        out_ref[rows + place : rows + place + 1, : ref.shape[1]] = ref[...]


def pack_weights(weight, vectors):
    rows, cols = weight.shape
    extra = -(-len(vectors) // 16) * 16
    return pl.pallas_call(
        pack_kernel,
        out_shape=jax.ShapeDtypeStruct((rows + extra, cols), weight.dtype),
        name="pack_weights",
    )(weight, *[v[None] for v in vectors])


def join_kernel(out_ref, up_ref, down_ref, all_ref):
    rows, width = out_ref.shape
    hidden_n = up_ref.shape[1]
    all_ref[:, :width] = out_ref[...]
    all_ref[:, width : width + hidden_n] = up_ref[...]
    for part in range(hidden_n // width):
        start = width + hidden_n + part * width
        all_ref[:, start : start + width] = down_ref[part * rows : (part + 1) * rows, :]


def join_weights(out_weight, up_weight, down_weight):
    rows, width = out_weight.shape
    return pl.pallas_call(
        join_kernel,
        out_shape=jax.ShapeDtypeStruct((rows, width + 2 * up_weight.shape[1]), out_weight.dtype),
        compiler_params=pltpu.CompilerParams(vmem_limit_bytes=vmem_cap),
        name="join_weights",
    )(out_weight, up_weight, down_weight)


def project_kernel(x_ref, weight_ref, bias_ref, q_ref, k_ref, v_ref, weight, *, part):
    shards = weight_ref.shape[0]
    width = x_ref.shape[1]

    @pl.when(pl.program_id(0) == 0)
    def _():
        for shard in range(shards):
            weight[shard * part : (shard + 1) * part, :] = weight_ref[shard, :part, :]

    x = x_ref[...]
    q_ref[...] = (dot(x, weight[:, :width]) + bias_ref[:, :width]).astype(bf16)
    k_ref[...] = dot(x, weight[:, width : 2 * width]).astype(bf16)
    v_ref[...] = (dot(x, weight[:, 2 * width :]) + bias_ref[:, width:]).astype(bf16)


def project(x, weight, bias):
    tokens, width = x.shape
    tile = min(512, tokens)
    row = pl.BlockSpec((tile, width), lambda i: (i, 0))
    shape = jax.ShapeDtypeStruct((tokens, width), bf16)
    return pl.pallas_call(
        functools.partial(project_kernel, part=width // weight.shape[0]),
        grid=(tokens // tile,),
        in_specs=[
            row,
            pl.BlockSpec(weight.shape, lambda i: (0, 0, 0), pipeline_mode=pl.Buffered(1)),
            pl.BlockSpec(bias.shape, lambda i: (0, 0)),
        ],
        out_specs=[row] * 3,
        out_shape=[shape] * 3,
        scratch_shapes=[pltpu.VMEM((width, weight.shape[2]), bf16)],
        compiler_params=pltpu.CompilerParams(vmem_limit_bytes=vmem_cap),
        cost_estimate=pl.CostEstimate(flops=0, bytes_accessed=tokens, transcendentals=0),
        name="project",
    )(x, weight, bias)


def grads_kernel(*refs, groups, extra, held):
    out_ref = refs[-1]
    start = 0
    for left, rights in groups:
        right = [refs[place][...] for place in rights]
        right = right[0] if len(right) == 1 else jnp.concatenate(right, axis=1)
        cols = right.shape[1]
        out_ref[:, start : start + cols] = dot(refs[left][...], right, cols_by_cols).astype(bf16)
        start += cols
    if extra:
        out_ref[:, start:] = jnp.transpose(refs[held - 1][...]).astype(bf16)


def weight_grads(groups, extra=None, after=()):
    arrays, places = [], []
    for left, rights in groups:
        places.append((len(arrays), tuple(range(len(arrays) + 1, len(arrays) + 1 + len(rights)))))
        arrays += [left] + list(rights)
    cols = sum(right.shape[1] for _, rights in groups for right in rights)
    if extra is not None:
        arrays.append(extra)
        cols += extra.shape[0]
    held = len(arrays)
    return pl.pallas_call(
        functools.partial(grads_kernel, groups=places, extra=extra is not None, held=held),
        in_specs=[pl.BlockSpec(memory_space=pltpu.VMEM)] * held
        + [pl.BlockSpec(memory_space=pl.ANY)] * len(after),
        out_shape=jax.ShapeDtypeStruct((groups[0][0].shape[1], cols), bf16),
        compiler_params=pltpu.CompilerParams(vmem_limit_bytes=vmem_cap),
        cost_estimate=pl.CostEstimate(flops=0, bytes_accessed=cols, transcendentals=0),
        name="weight_grads",
    )(*arrays, *after)


def input_kernel(*refs, part, parts_n):
    weight_ref, pre_ref = refs[0], refs[1]
    out_ref, weight = refs[-2], refs[-1]
    shards = weight_ref.shape[0]

    @pl.when(pl.program_id(0) == 0)
    def _():
        for shard in range(shards):
            weight[shard * part : (shard + 1) * part, :] = weight_ref[shard, :part, :]

    grads = jnp.concatenate([ref[...] for ref in refs[2 : 2 + parts_n]], axis=1)
    out_ref[...] = (pre_ref[...] + dot(grads, weight[...], rows_by_rows)).astype(bf16)


def input_gradient(weight, grad_pre, parts, after):
    tokens, width = grad_pre.shape
    tile = min(512, tokens)

    def row(n):
        return pl.BlockSpec((tile, n), lambda i: (i, 0))

    return pl.pallas_call(
        functools.partial(input_kernel, part=width // weight.shape[0], parts_n=len(parts)),
        grid=(tokens // tile,),
        in_specs=[pl.BlockSpec(weight.shape, lambda i: (0, 0, 0), pipeline_mode=pl.Buffered(1))]
        + [row(width)]
        + [row(part.shape[1]) for part in parts]
        + [pl.BlockSpec(memory_space=pl.ANY)] * len(after),
        out_specs=row(width),
        out_shape=jax.ShapeDtypeStruct((tokens, width), bf16),
        scratch_shapes=[pltpu.VMEM((width, weight.shape[2]), bf16)],
        compiler_params=pltpu.CompilerParams(vmem_limit_bytes=vmem_cap),
        cost_estimate=pl.CostEstimate(flops=0, bytes_accessed=tokens, transcendentals=0),
        name="input_gradient",
    )(weight, grad_pre, *parts, *after)


def token_kernel(
    attended_ref,
    x_ref,
    cot_ref,
    weights_ref,
    vec_ref,
    bias_up_ref,
    out_ref,
    hidden_ref,
    active_ref,
    grad_mlp_ref,
    grad_upper_ref,
    grad_pre_ref,
    grad_branch_ref,
    grad_attended_ref,
    sums_ref,
    sums_up_ref,
    weight_out,
    weight_up,
    weight_down,
    slope,
    arrived,
):
    shards, part = weights_ref.shape[:2]
    width, hidden_n = weight_up.shape
    chunks = hidden_n // width

    @pl.when(pl.program_id(0) == 0)
    def _():
        copies = []
        for shard in range(shards):
            rows = pl.ds(shard * part, part)
            mine = weights_ref.at[shard]
            copies.append((mine.at[:, pl.ds(0, width)], weight_out.at[rows, :]))
            copies.append((mine.at[:, pl.ds(width, hidden_n)], weight_up.at[rows, :]))
            for chunk in range(chunks):
                start = width + hidden_n + chunk * width
                rows = pl.ds((shard * chunks + chunk) * part, part)
                copies.append((mine.at[:, pl.ds(start, width)], weight_down.at[rows, :]))
        copies = [
            pltpu.make_async_copy(source, target, arrived.at[place])
            for place, (source, target) in enumerate(copies)
        ]
        for copy in copies:
            copy.start()
        for copy in copies:
            copy.wait()
        sums_ref[...] = jnp.zeros_like(sums_ref)
        sums_up_ref[...] = jnp.zeros_like(sums_up_ref)

    bias_out, gain_one, shift_one, bias_down, gain_two, shift_two = [
        vec_ref[place : place + 1, :] for place in range(6)
    ]

    def mean(value):
        return jnp.mean(value, axis=1, keepdims=True)

    def add_to(place, value):
        sums_ref[place : place + 1, :] += jnp.sum(value.astype(f32), axis=0, keepdims=True)

    def normed(value):
        centred = value - mean(value)
        inverse = lax.rsqrt(mean(centred * centred) + eps_norm)
        return centred * inverse, inverse

    def norm_backward(incoming, normed_value, inverse, gain):
        scaled = incoming * gain
        centred = scaled - mean(scaled) - normed_value * mean(scaled * normed_value)
        return centred * inverse

    branch = dot(attended_ref[...], weight_out[...]) + bias_out
    normed_one, inverse_one = normed(x_ref[...].astype(f32) + branch)
    hidden = normed_one * gain_one + shift_one
    hidden_low = hidden.astype(bf16)
    hidden_ref[...] = hidden_low
    mlp_out = jnp.zeros_like(hidden)
    for chunk in range(chunks):
        cols = slice(chunk * width, (chunk + 1) * width)
        upper = dot(hidden_low, weight_up[:, cols]) + bias_up_ref[:, cols]
        share = 0.5 * (1.0 + lax.erf(upper * 0.5**0.5))
        density = jnp.exp(-0.5 * upper * upper) * (2.0 * jnp.pi) ** -0.5
        active = (upper * share).astype(bf16)
        active_ref[:, cols] = active
        slope[:, cols] = share + upper * density
        mlp_out = mlp_out + dot(active, weight_down[cols, :])
    normed_two, inverse_two = normed(hidden + (mlp_out + bias_down))
    out_ref[...] = (normed_two * gain_two + shift_two).astype(bf16)

    incoming = cot_ref[...].astype(f32)
    grad_sum = norm_backward(incoming, normed_two, inverse_two, gain_two)
    grad_mlp = grad_sum.astype(bf16)
    grad_mlp_ref[...] = grad_mlp
    add_to(5, incoming)
    add_to(4, incoming * normed_two)
    add_to(3, grad_mlp)
    grad_hidden = grad_sum
    for chunk in range(chunks):
        cols = slice(chunk * width, (chunk + 1) * width)
        grad_active = dot(grad_mlp, weight_down[cols, :], rows_by_rows)
        grad_upper = (grad_active * slope[:, cols]).astype(bf16)
        grad_upper_ref[:, cols] = grad_upper
        sums_up_ref[0:1, cols] += jnp.sum(grad_upper.astype(f32), axis=0, keepdims=True)
        grad_hidden = grad_hidden + dot(grad_upper, weight_up[:, cols], rows_by_rows)
    grad_pre = norm_backward(grad_hidden, normed_one, inverse_one, gain_one)
    grad_pre_ref[...] = grad_pre
    grad_branch = grad_pre.astype(bf16)
    grad_branch_ref[...] = grad_branch
    add_to(2, grad_hidden)
    add_to(1, grad_hidden * normed_one)
    add_to(0, grad_branch)
    grad_attended_ref[...] = dot(grad_branch, weight_out[...], rows_by_rows).astype(bf16)


def token_parts(attended, x, cotangent, weights, vecs, bias_up):
    tokens, width = x.shape
    shards, part, cols = weights.shape
    hidden_n = (cols - width) // 2
    tile = 256

    def row(n):
        return pl.BlockSpec((tile, n), lambda i: (i, 0))

    def fixed(shape):
        return pl.BlockSpec(shape, lambda i: (0, 0))

    def shape(n, kind=bf16):
        return jax.ShapeDtypeStruct((tokens, n), kind)

    copies = shards * (2 + hidden_n // width)
    return pl.pallas_call(
        token_kernel,
        grid=(tokens // tile,),
        in_specs=[row(width)] * 3
        + [pl.BlockSpec(memory_space=pl.ANY), fixed(vecs.shape), fixed(bias_up.shape)],
        out_specs=[
            row(width),
            row(width),
            row(hidden_n),
            row(width),
            row(hidden_n),
            row(width),
            row(width),
            row(width),
            fixed((8, width)),
            fixed((8, hidden_n)),
        ],
        out_shape=[
            shape(width),
            shape(width),
            shape(hidden_n),
            shape(width),
            shape(hidden_n),
            shape(width, f32),
            shape(width),
            shape(width),
            jax.ShapeDtypeStruct((8, width), f32),
            jax.ShapeDtypeStruct((8, hidden_n), f32),
        ],
        scratch_shapes=[
            pltpu.VMEM((width, width), bf16),
            pltpu.VMEM((width, hidden_n), bf16),
            pltpu.VMEM((hidden_n, width), bf16),
            pltpu.VMEM((tile, hidden_n), f32),
            pltpu.SemaphoreType.DMA((copies,)),
        ],
        compiler_params=pltpu.CompilerParams(vmem_limit_bytes=vmem_cap),
        cost_estimate=pl.CostEstimate(flops=0, bytes_accessed=tokens, transcendentals=0),
        name="token_parts",
    )(attended, x, cotangent, weights, vecs, bias_up)


def body(
    inputs,
    segments,
    random_blocks,
    cotangent,
    qkv_weight,
    qv_bias,
    out_weight,
    out_bias,
    norm1_gain,
    norm1_bias,
    up_weight,
    up_bias,
    down_weight,
    down_bias,
    norm2_gain,
    norm2_bias,
):
    seq_count, run, width = inputs.shape
    per_dev, head_count, rand_count = random_blocks.shape[1:]
    block = run // per_dev
    head_size = width // head_count
    dp_count = lax.axis_size("dp")
    ctx_count = lax.axis_size("ctx")
    ctx_index = lax.axis_index("ctx")
    team = ctx_count // seq_count
    tokens = seq_count * run

    x = swap_pieces(inputs, "ctx", team).reshape(tokens, width)
    lists = swap_pieces(tied(random_blocks.reshape(seq_count, 1, -1), x), "ctx", team)

    def back_to_runs(rows):
        return swap_pieces(rows.reshape(seq_count, run, width), "ctx", team)

    vectors = (qv_bias, out_bias, norm1_gain, norm1_bias, up_bias, down_bias, norm2_gain, norm2_bias)
    sizes = [v.shape[0] for v in vectors]
    qkv_rows, qkv_cols = qkv_weight.shape
    first = lax.all_gather(pack_weights(qkv_weight, vectors), "dp", axis=0)
    others = lax.all_gather(join_weights(out_weight, up_weight, down_weight), "dp", axis=0)

    def vector(place):
        return first[:, qkv_rows + place, : sizes[place]].reshape(1, -1).astype(f32)

    bias_qv, bias_up = vector(0), vector(4)
    vecs = first[:, qkv_rows + 1 : qkv_rows + 8, :qkv_rows].transpose(1, 0, 2).reshape(7, width)
    vecs = jnp.concatenate([vecs[:3], vecs[4:], jnp.zeros_like(vecs[:2])], axis=0).astype(f32)

    seq_index = ctx_index // team
    seg = lax.dynamic_index_in_dim(segments, seq_index, 0, keepdims=False)
    lists = lists.reshape(seq_count, per_dev, head_count, rand_count)
    if team > 1:
        team_index = ctx_index % team
        held = -(-head_count // (2 * team)) * 2
        spare = held * team - head_count
        lists = jnp.stack(share_pieces(lists, "ctx", 1, team)).transpose(1, 0, 2, 3, 4)
        lists = jnp.pad(lists.reshape(-1, head_count, rand_count), ((0, 0), (0, spare), (0, 0)))
        lists = lax.dynamic_slice_in_dim(lists, team_index * held, held, 1)
    else:
        lists = lists.reshape(-1, head_count, rand_count)
    features = mask_features(seg, lists, block)

    def to_heads(rows):
        if team == 1:
            return rows
        rows = jnp.pad(rows, ((0, 0), (0, spare * head_size)))
        part = swap_pieces(rows.reshape(tokens, team, -1).transpose(1, 0, 2), "ctx", 1)
        part = part.reshape(team, seq_count, run, -1).transpose(1, 0, 2, 3)
        return part.reshape(team * tokens, -1)

    def to_tokens(part):
        if team == 1:
            return part
        part = part.reshape(seq_count, team, run, -1).transpose(1, 0, 2, 3)
        rows = swap_pieces(part.reshape(team, tokens, -1), "ctx", 1)
        return rows.transpose(1, 0, 2).reshape(tokens, -1)[:, :width]

    queries, keys, values = project(x, first, bias_qv)
    grad_result = swap_pieces(tied(cotangent, x), "ctx", team).reshape(tokens, width)
    heads = tuple(to_heads(part) for part in (queries, keys, values))
    attended = attend(forward_kernel, heads, features, 1, head_size, "attend_forward")[0]
    attended = to_tokens(attended)
    parts = token_parts(attended, x, grad_result, others, vecs, bias_up)
    result, hidden_low, active, grad_mlp, grad_upper, grad_pre, grad_branch, grad_att, sums, sums_up = parts

    def weight_grad(left, right):
        return dot(left, right, cols_by_cols).astype(bf16)

    down_grad = weight_grad(active, grad_mlp)
    down_part = scattered(down_grad)
    up_grad = weight_grad(hidden_low, tied(grad_upper, down_grad))
    up_part = scattered(up_grad)
    layer_out = back_to_runs(tied(result, up_grad))
    back_heads = heads + (to_heads(grad_att),)
    pair_count = back_heads[0].shape[1] // lanes_n
    back = attend(backward_kernel, back_heads, features, 3, head_size, "attend_backward", (up_grad,))
    if team > 1:
        back = [to_tokens(array) for array in back[:3]]
        back.append(jnp.stack([jnp.sum(back[i].astype(f32), axis=0) for i in (0, 2)]))
    *back, bias_sums = back
    def shard_rows(values):
        return values.reshape(dp_count, -1, qkv_rows).transpose(1, 0, 2).reshape(-1, width)

    side = [shard_rows(bias_sums[:2].reshape(-1)), sums[:6], shard_rows(sums_up[0])]
    side_rows = [part.shape[0] for part in side]
    side_n = -(-sum(side_rows) // lanes_n) * lanes_n
    side.append(jnp.zeros((side_n - sum(side_rows), width), f32))
    down, up = Chain(down_part, "ctx"), Chain(up_part, "ctx")
    sent = down.begin(back[0])
    groups = [(attended, [grad_branch]), (x, back)]
    rest = Chain(weight_grads(groups, jnp.concatenate(side, axis=0), (sent, layer_out)), "dp")
    sent = rest.begin(rest.value)
    result = input_gradient(first, grad_pre, back, (sent,))
    rest.end(result)
    sent = rest.begin(result)
    input_grad = back_to_runs(tied(result, sent))
    down.end(sent)
    sent = down.begin(sent)
    up.begin(sent)
    half = len(stages_of(ctx_count))
    while len(up.plan) > half + 1 or len(down.plan) > half + 1:
        for chain in (down, up):
            if len(chain.plan) > half + 1:
                chain.begin(chain.end())
    pieces = jnp.concatenate([down.end(), up.end().reshape(-1, width)], axis=0)
    pieces = lax.all_gather(pieces, "ctx", axis=0)
    last = Chain(rest.end(), "ctx")
    last.begin(last.value)
    while last.open():
        value = last.end()
        if last.open():
            last.begin(value)
    bits = len(stages_of(ctx_count))
    pieces = pieces.reshape((2,) * bits + pieces.shape[1:])
    pieces = pieces.transpose(tuple(reversed(range(bits))) + (bits, bits + 1))
    pieces = pieces.reshape((ctx_count,) + pieces.shape[bits:])
    down_rows = down_part.shape[0] // ctx_count
    down_total = pieces[:, :down_rows].reshape(down_part.shape)
    up_total = pieces[:, down_rows:].reshape(up_part.shape)
    total = last.value.astype(f32)
    out_total, qkv_total = total[:, :width], total[:, width : width + qkv_cols]
    flat = total[:, width + qkv_cols : width + qkv_cols + sum(side_rows)].T
    starts = [0, 2, 3, 4, 8, 5, 6, 7]
    vec_totals = [
        flat[start : start + size // qkv_rows].reshape(-1) for start, size in zip(starts, sizes)
    ]
    return (
        layer_out,
        input_grad,
        qkv_total,
        vec_totals[0],
        out_total,
        vec_totals[1],
        vec_totals[2],
        vec_totals[3],
        up_total.astype(f32),
        vec_totals[4],
        down_total.astype(f32),
        vec_totals[5],
        vec_totals[6],
        vec_totals[7],
    )


def solution(mesh):
    tokens = P("dp", "ctx", None)
    matrix, vector = P("dp", None), P("dp")
    weights = (matrix, vector, matrix, vector, vector, vector, matrix, vector, matrix, vector, vector, vector)
    return jax.shard_map(
        body,
        mesh=mesh,
        in_specs=(tokens, matrix, P("dp", "ctx", None, None), tokens) + weights,
        out_specs=(tokens, tokens) + weights,
        check_vma=False,
    )
```

```python
import functools

import jax
import jax.numpy as jnp
from jax import lax
from jax.experimental import pallas as pl
from jax.experimental.pallas import tpu as pltpu
from jax.sharding import PartitionSpec as P

f32, bf16 = jnp.float32, jnp.bfloat16
eps_norm = 1e-12
far = 1e30
doc_min = 200
lanes_n = 128
vmem_cap = 56 * 2**20


def swap_pieces(pieces, axis, stride):
    count, size = pieces.shape[0], lax.axis_size(axis)
    groups = None
    if count < size:
        span = stride * count
        starts = [base + offset for base in range(0, size, span) for offset in range(stride)]
        groups = [[start + i * stride for i in range(count)] for start in starts]
    return lax.all_to_all(pieces, axis, 0, 0, axis_index_groups=groups, tiled=True)


def share_pieces(piece, axis, count):
    size = lax.axis_size(axis)
    member = lax.axis_index(axis) % count
    came, stride = piece[None], 1
    while stride < count:
        other = lax.ppermute(came, axis, [(i, i ^ stride) for i in range(size)])
        upper = (member // stride) % 2 == 1
        came = jnp.concatenate([jnp.where(upper, other, came), jnp.where(upper, came, other)], axis=0)
        stride *= 2
    return came


def tied(value, *deps):
    def nothing(*refs):
        pass

    return pl.pallas_call(
        nothing,
        in_specs=[pl.BlockSpec(memory_space=pl.ANY)] * (1 + len(deps)),
        out_specs=pl.BlockSpec(memory_space=pl.ANY),
        out_shape=jax.ShapeDtypeStruct(value.shape, value.dtype),
        input_output_aliases={0: 0},
        name="tied",
    )(value, *deps)


def added(terms):
    if len(terms) == 1:
        return terms[0]
    total = terms[0].astype(f32)
    for term in terms[1:]:
        total = total + term.astype(f32)
    return total.astype(bf16)


class Chain:
    def __init__(self, parts, axis="ctx"):
        self.parts = parts
        strides, stride = [], 1
        while stride < lax.axis_size(axis):
            strides.append(stride)
            stride *= 2
        self.axis = axis
        self.plan = [(stride, True) for stride in strides]
        if axis == "ctx":
            self.plan += [(stride, False) for stride in reversed(strides)]

    def halves(self, stride):
        member = (lax.axis_index(self.axis) // stride) % 2

        def half(which):
            columns = []
            for terms in self.parts:
                rows = terms[0].shape[0] // 2
                cut = [lax.dynamic_slice_in_dim(term, which * rows, rows, 0) for term in terms]
                columns.append(added(cut))
            return columns[0] if len(columns) == 1 else jnp.concatenate(columns, axis=1)

        return half(member), half(1 - member)

    def begin(self, *after):
        stride, adds = self.plan[0]
        if adds:
            self.kept, sent = self.halves(stride)
            sent = tied(sent, *after)
        else:
            sent = tied(added(self.parts[0]), *after)
            self.kept = sent
        size = lax.axis_size(self.axis)
        self.came = lax.ppermute(sent, self.axis, [(i, i ^ stride) for i in range(size)])
        return sent

    def end(self, *after):
        stride, adds = self.plan.pop(0)
        came = tied(self.came, *after) if after else self.came
        if adds:
            self.parts = [[self.kept, came]]
        else:
            upper = (lax.axis_index(self.axis) // stride) % 2 == 1
            pair = [jnp.where(upper, came, self.kept), jnp.where(upper, self.kept, came)]
            self.parts = [[jnp.concatenate(pair, axis=0)]]
        return self.parts[0]

    def next(self, *after):
        self.end()
        return self.begin(*after)

    def open(self):
        return len(self.plan) > 0


class Scatter:
    def __init__(self, kept, sent):
        self.kept, self.came, self.stride = kept, None, 1
        self.sent = sent

    def begin(self, *after):
        size = lax.axis_size("dp")
        sent = tied(self.sent, *after)
        self.came = lax.ppermute(sent, "dp", [(i, i ^ self.stride) for i in range(size)])
        return sent

    def end(self, *after):
        came = tied(self.came, *after) if after else self.came
        self.stride *= 2
        if self.stride == lax.axis_size("dp"):
            return [self.kept, came]
        rows = self.kept.shape[0] // 2
        self.sent = added([self.kept[rows:], came[rows:]])
        self.kept = added([self.kept[:rows], came[:rows]])
        return None


def copied(value, *deps):
    def copy(value_ref, *refs):
        refs[-1][...] = value_ref[...]

    return pl.pallas_call(
        copy,
        in_specs=[pl.BlockSpec(memory_space=pltpu.VMEM)]
        + [pl.BlockSpec(memory_space=pl.ANY)] * len(deps),
        out_shape=jax.ShapeDtypeStruct(value.shape, value.dtype),
        name="copied",
    )(value, *deps)


def scattered(grad):
    return lax.psum_scatter(grad, "dp", scatter_dimension=0, tiled=True)


def mask_features(seg, rand, block):
    tokens = seg.shape[0]
    blocks, heads = rand.shape[:2]
    seg_limit = tokens // doc_min + 1
    used = seg_limit + 2 * blocks
    width = -(-used // lanes_n) * lanes_n
    ids = jnp.arange(blocks, dtype=jnp.int32)

    def hot(values):
        return (values[..., None] == ids).astype(jnp.int32)

    near = hot(ids - 1) + hot(ids) + hot(ids + 1) + hot(ids * 0) + hot(ids * 0 + blocks - 1)
    counts = near[:, None, :] + jnp.sum(hot(rand), axis=2)
    edge = (ids == 0) | (ids == blocks - 1)
    counts = jnp.where(edge[:, None, None], 1, counts).transpose(1, 2, 0)
    log_count = jnp.log(jnp.maximum(counts, 1).astype(f32))
    high = log_count.astype(bf16).astype(f32)
    low = jnp.where(counts > 0, log_count - high, 0.0)
    high = jnp.where(counts > 0, high, -far)
    table = jnp.concatenate(
        [
            jnp.zeros((heads, blocks, seg_limit), f32),
            high,
            low,
            jnp.zeros((heads, blocks, width - used), f32),
        ],
        axis=2,
    )
    lane = jnp.arange(width, dtype=jnp.int32)[None]
    own = (jnp.arange(tokens, dtype=jnp.int32) // block)[:, None]
    is_seg = lane < seg_limit
    same = lane == seg[:, None]
    key_feat = jnp.where(is_seg & same, 1.0, 0.0).astype(bf16)
    own_lane = (lane - seg_limit == own) | (lane - seg_limit - blocks == own)
    query_feat = jnp.where(
        is_seg, jnp.where(same, 0.0, -far), jnp.where(own_lane, 1.0, 0.0)
    ).astype(bf16)
    near = -(-seg_limit // lanes_n) * lanes_n
    return key_feat[:, :near], query_feat[:, :near], table


def fill_keys(k_ref, key_feat_ref, table_ref, keys):
    tokens, near = key_feat_ref.shape
    blocks, width = table_ref.shape[1:]
    feat = key_feat_ref[...].astype(f32).reshape(blocks, tokens // blocks, near)
    for side in range(2):
        rows = table_ref[side][:, None, :]
        both = (feat + rows[..., :near]).reshape(tokens, near)
        keys[side, :, :lanes_n] = k_ref[...]
        keys[side, :, lanes_n : lanes_n + near] = both.astype(bf16)
        if width > near:
            rest = jnp.broadcast_to(rows[..., near:], (blocks, tokens // blocks, width - near))
            keys[side, :, lanes_n + near :] = rest.reshape(tokens, width - near).astype(bf16)


def query_lanes(near_feat, start, tokens, blocks, width):
    rows, near = near_feat.shape
    if width == near:
        return near_feat
    shape = (rows, width - near)
    lane = lax.broadcasted_iota(jnp.int32, shape, 1) + near - (tokens // doc_min + 1)
    own = (lax.broadcasted_iota(jnp.int32, shape, 0) + start) // (tokens // blocks)
    rest = jnp.where((lane == own) | (lane - blocks == own), 1.0, 0.0).astype(bf16)
    return jnp.concatenate([near_feat, rest], axis=1)


rows_by_rows = (((1,), (1,)), ((), ()))
cols_by_cols = (((0,), (0,)), ((), ()))


def dot(left, right, dims=(((1,), (0,)), ((), ()))):
    return lax.dot_general(left, right, dims, preferred_element_type=f32)


def forward_kernel(
    q_ref, k_ref, v_ref, key_feat_ref, query_feat_ref, table_ref, out_ref, keys, vals, *, half, tile
):
    tokens = q_ref.shape[0]
    fill_keys(k_ref, key_feat_ref, table_ref, keys)
    vals[:, :lanes_n] = v_ref[...]
    vals[:, lanes_n:] = jnp.ones((tokens, lanes_n), bf16)

    @pl.loop(0, tokens // tile)
    def _(step):
        rows = pl.ds(pl.multiple_of(step * tile, tile), tile)
        q = q_ref[rows, :] * bf16(half**-0.5)
        side_of = lax.broadcasted_iota(jnp.int32, (tile, lanes_n), 1) // half
        feat = query_lanes(query_feat_ref[rows, :], step * tile, tokens, *table_ref.shape[1:])
        scores = [
            dot(
                jnp.concatenate([jnp.where(side_of == side, q, bf16(0)), feat], axis=1),
                keys[side],
                rows_by_rows,
            )
            for side in range(2)
        ]
        outs = []
        for score in scores:
            weights = jnp.exp(score - jnp.max(score, axis=1, keepdims=True)).astype(bf16)
            mixed = dot(weights, vals[...])
            outs.append(mixed[:, :lanes_n] / mixed[:, lanes_n:])
        out_ref[rows, :] = jnp.where(side_of == 0, outs[0], outs[1]).astype(bf16)


def backward_kernel(
    q_ref,
    k_ref,
    v_ref,
    grad_ref,
    key_feat_ref,
    query_feat_ref,
    table_ref,
    dq_ref,
    dk_ref,
    dv_ref,
    sums_ref,
    keys,
    dk_sum,
    dv_sum,
    *,
    half,
    tile,
):
    tokens = q_ref.shape[0]
    fill_keys(k_ref, key_feat_ref, table_ref, keys)
    dk_sum[...] = jnp.zeros_like(dk_sum)
    dv_sum[...] = jnp.zeros_like(dv_sum)
    sums_ref[...] = jnp.zeros_like(sums_ref)

    @pl.loop(0, tokens // tile)
    def _(step):
        rows = pl.ds(pl.multiple_of(step * tile, tile), tile)
        q_pair = q_ref[rows, :] * bf16(half**-0.5)
        grad_pair = grad_ref[rows, :]
        side_of = lax.broadcasted_iota(jnp.int32, (tile, lanes_n), 1) // half
        feat = query_lanes(query_feat_ref[rows, :], step * tile, tokens, *table_ref.shape[1:])
        queries = [jnp.where(side_of == side, q_pair, bf16(0)) for side in range(2)]
        grads = [jnp.where(side_of == side, grad_pair, bf16(0)) for side in range(2)]
        probs, dscores = [], []
        for side in range(2):
            wide = jnp.concatenate([queries[side], feat], axis=1)
            scores = dot(wide, keys[side], rows_by_rows)
            dprobs = dot(grads[side], v_ref[...], rows_by_rows)
            raw = jnp.exp(scores - jnp.max(scores, axis=1, keepdims=True))
            prob = raw * (1.0 / jnp.sum(raw, axis=1, keepdims=True))
            both = prob * dprobs
            dscore = both - prob * jnp.sum(both, axis=1, keepdims=True)
            probs.append(prob.astype(bf16))
            dscores.append(dscore.astype(bf16))
        dv_sum[...] += dot(
            jnp.concatenate(probs, axis=0), jnp.concatenate(grads, axis=0), cols_by_cols
        )
        dk_sum[...] += dot(
            jnp.concatenate(dscores, axis=0), jnp.concatenate(queries, axis=0), cols_by_cols
        )
        dqs = [dot(dscore, k_ref[...]) for dscore in dscores]
        dq = (jnp.where(side_of == 0, dqs[0], dqs[1]) * half**-0.5).astype(bf16)
        dq_ref[rows, :] = dq
        sums_ref[0:1, :] += jnp.sum(dq.astype(f32), axis=0, keepdims=True)

    dk_ref[...] = dk_sum[...].astype(bf16)
    dv = dv_sum[...].astype(bf16)
    dv_ref[...] = dv
    sums_ref[1:2, :] = jnp.sum(dv.astype(f32), axis=0, keepdims=True)


def attend(kernel, arrays, features, outs, half, name, after=(), first=0, count=None):
    tokens, width = arrays[0].shape
    key_feat, query_feat, table = features
    count = width // lanes_n if count is None else count
    near, feat_width = key_feat.shape[1], table.shape[2]
    tile = tokens if tokens <= 1024 else 32
    once = {"pipeline_mode": pl.Buffered(1)} if count == 1 else {}
    pair = pl.BlockSpec((tokens, lanes_n), lambda p: (0, p + first), **once)
    pair_out = pl.BlockSpec((tokens, lanes_n), lambda p: (0, p), **once)
    whole = pl.BlockSpec((tokens, near), lambda p: (0, 0), pipeline_mode=pl.Buffered(1))
    shape = jax.ShapeDtypeStruct((tokens, count * lanes_n), bf16)
    scratch = [pltpu.VMEM((2, tokens, lanes_n + feat_width), bf16)]
    if outs == 1:
        scratch = scratch + [pltpu.VMEM((tokens, 2 * lanes_n), bf16)]
    else:
        scratch = scratch + [pltpu.VMEM((tokens, lanes_n), f32)] * 2

    def run(*refs):
        held = len(arrays) + 3
        kernel(*refs[:held], *refs[held + len(after) :], half=half, tile=tile)

    return pl.pallas_call(
        run,
        grid=(count,),
        in_specs=[pair] * len(arrays)
        + [whole, whole]
        + [pl.BlockSpec((2,) + table.shape[1:], lambda p: (p + first, 0, 0))]
        + [pl.BlockSpec(memory_space=pl.ANY)] * len(after),
        out_specs=[pair_out] * outs + [pl.BlockSpec((8, lanes_n), lambda p: (0, p))] * (outs > 1),
        out_shape=[shape] * outs
        + [jax.ShapeDtypeStruct((8, count * lanes_n), f32)] * (outs > 1),
        scratch_shapes=scratch,
        compiler_params=pltpu.CompilerParams(vmem_limit_bytes=vmem_cap),
        cost_estimate=pl.CostEstimate(flops=0, bytes_accessed=tokens, transcendentals=0),
        name=name,
    )(*arrays, key_feat, query_feat, table, *after)


def pack_kernel(weight_ref, *refs):
    out_ref = refs[-1]
    rows = weight_ref.shape[0]
    out_ref[:rows, :] = weight_ref[...]
    out_ref[rows:, :] = jnp.zeros_like(out_ref[rows:, :])
    for place, ref in enumerate(refs[:-1]):
        out_ref[rows + place : rows + place + 1, : ref.shape[0]] = ref[...].reshape(1, -1)


def pack_weights(weight, vectors):
    rows, cols = weight.shape
    extra = -(-len(vectors) // 16) * 16
    return pl.pallas_call(
        pack_kernel,
        out_shape=jax.ShapeDtypeStruct((rows + extra, cols), weight.dtype),
        name="pack_weights",
    )(weight, *vectors)


def join_kernel(out_ref, up_ref, down_ref, all_ref):
    rows, width = out_ref.shape
    hidden_n = up_ref.shape[1]
    all_ref[:, :width] = out_ref[...]
    all_ref[:, width : width + hidden_n] = up_ref[...]
    for part in range(hidden_n // width):
        start = width + hidden_n + part * width
        all_ref[:, start : start + width] = down_ref[part * rows : (part + 1) * rows, :]


def join_weights(out_weight, up_weight, down_weight):
    rows, width = out_weight.shape
    return pl.pallas_call(
        join_kernel,
        out_shape=jax.ShapeDtypeStruct((rows, width + 2 * up_weight.shape[1]), out_weight.dtype),
        compiler_params=pltpu.CompilerParams(vmem_limit_bytes=vmem_cap),
        name="join_weights",
    )(out_weight, up_weight, down_weight)


def project_kernel(x_ref, weight_ref, bias_ref, q_ref, k_ref, v_ref, weight, *, part):
    shards = weight_ref.shape[0]
    width = x_ref.shape[1]

    @pl.when(pl.program_id(0) == 0)
    def _():
        for shard in range(shards):
            weight[shard * part : (shard + 1) * part, :] = weight_ref[shard, :part, :]

    x = x_ref[...]
    q_ref[...] = (dot(x, weight[:, :width]) + bias_ref[:, :width]).astype(bf16)
    k_ref[...] = dot(x, weight[:, width : 2 * width]).astype(bf16)
    v_ref[...] = (dot(x, weight[:, 2 * width :]) + bias_ref[:, width:]).astype(bf16)


def project(x, weight, bias):
    tokens, width = x.shape
    tile = min(512, tokens)
    row = pl.BlockSpec((tile, width), lambda i: (i, 0))
    shape = jax.ShapeDtypeStruct((tokens, width), bf16)
    return pl.pallas_call(
        functools.partial(project_kernel, part=width // weight.shape[0]),
        grid=(tokens // tile,),
        in_specs=[
            row,
            pl.BlockSpec(weight.shape, lambda i: (0, 0, 0), pipeline_mode=pl.Buffered(1)),
            pl.BlockSpec(bias.shape, lambda i: (0, 0)),
        ],
        out_specs=[row] * 3,
        out_shape=[shape] * 3,
        scratch_shapes=[pltpu.VMEM((width, weight.shape[2]), bf16)],
        compiler_params=pltpu.CompilerParams(vmem_limit_bytes=vmem_cap),
        cost_estimate=pl.CostEstimate(flops=0, bytes_accessed=tokens, transcendentals=0),
        name="project",
    )(x, weight, bias)


def sort_shards(place_ref, grad, kept_ref, sent_ref, shards, block, block_n):
    rows = grad.shape[0] // shards
    for shard in range(shards):
        turn = place_ref[0] ^ shard
        start = pl.multiple_of(((turn // 2) * block_n + block) * rows, rows)
        piece = grad[shard * rows : (shard + 1) * rows].astype(bf16)

        @pl.when(turn % 2 == 0)
        def _():
            kept_ref[pl.ds(start, rows), : grad.shape[1]] = piece

        @pl.when(turn % 2 == 1)
        def _():
            sent_ref[pl.ds(start, rows), : grad.shape[1]] = piece


def grads_kernel(place_ref, *refs, groups, held, shards):
    kept_ref, sent_ref = refs[-2:]
    grads = []
    for left, rights in groups:
        right = [refs[place][...] for place in rights]
        right = right[0] if len(right) == 1 else jnp.concatenate(right, axis=1)
        grads.append(dot(refs[left][...], right, cols_by_cols).astype(bf16))
    grads.append(jnp.transpose(refs[held - 1][...]).astype(bf16))
    sort_shards(place_ref, jnp.concatenate(grads, axis=1), kept_ref, sent_ref, shards, 0, 1)


def weight_grads(place, groups, extra, shards, after=()):
    arrays, places = [], []
    for left, rights in groups:
        places.append((len(arrays), tuple(range(len(arrays) + 1, len(arrays) + 1 + len(rights)))))
        arrays += [left] + list(rights)
    arrays.append(extra)
    cols = sum(right.shape[1] for _, rights in groups for right in rights) + extra.shape[0]
    held = len(arrays)
    half = jax.ShapeDtypeStruct((groups[0][0].shape[1] // 2, cols), bf16)
    return pl.pallas_call(
        functools.partial(grads_kernel, groups=places, held=held, shards=shards),
        in_specs=[pl.BlockSpec(memory_space=pltpu.SMEM)]
        + [pl.BlockSpec(memory_space=pltpu.VMEM)] * held
        + [pl.BlockSpec(memory_space=pl.ANY)] * len(after),
        out_shape=[half] * 2,
        compiler_params=pltpu.CompilerParams(vmem_limit_bytes=vmem_cap),
        cost_estimate=pl.CostEstimate(flops=0, bytes_accessed=cols, transcendentals=0),
        name="weight_grads",
    )(place, *arrays, *after)


def wide_grad_kernel(place_ref, left_ref, right_ref, *refs, shards):
    grad = dot(left_ref[...], right_ref[...], cols_by_cols)
    sort_shards(
        place_ref, grad, refs[-2], refs[-1], shards, pl.program_id(0), pl.num_programs(0)
    )


def wide_grad(place, left, right, shards, after=()):
    tokens, rows = left.shape
    runs = right.shape[1] // rows
    half = (rows * runs // 2, rows)
    whole = pl.BlockSpec(half, lambda i: (0, 0))
    return pl.pallas_call(
        functools.partial(wide_grad_kernel, shards=shards),
        grid=(runs,),
        in_specs=[
            pl.BlockSpec(memory_space=pltpu.SMEM),
            pl.BlockSpec((tokens, rows), lambda i: (0, 0)),
            pl.BlockSpec((tokens, rows), lambda i: (0, i)),
        ]
        + [pl.BlockSpec(memory_space=pl.ANY)] * len(after),
        out_specs=[whole] * 2,
        out_shape=[jax.ShapeDtypeStruct(half, bf16)] * 2,
        compiler_params=pltpu.CompilerParams(vmem_limit_bytes=vmem_cap),
        cost_estimate=pl.CostEstimate(flops=0, bytes_accessed=rows, transcendentals=0),
        name="wide_grad",
    )(place, left, right, *after)


def matrix_grad_kernel(left_ref, right_ref, *refs):
    refs[-1][...] = dot(left_ref[...], right_ref[...], cols_by_cols).astype(bf16)


def matrix_grad(left, right, after=()):
    tokens, rows = left.shape
    cols = right.shape[1]
    run = min(rows, cols)
    tall = rows > cols

    def taken(yes):
        return pl.BlockSpec((tokens, run), (lambda i: (0, i)) if yes else (lambda i: (0, 0)))

    return pl.pallas_call(
        matrix_grad_kernel,
        grid=(max(rows, cols) // run,),
        in_specs=[taken(tall), taken(not tall)] + [pl.BlockSpec(memory_space=pl.ANY)] * len(after),
        out_specs=pl.BlockSpec((run, run), (lambda i: (i, 0)) if tall else (lambda i: (0, i))),
        out_shape=jax.ShapeDtypeStruct((rows, cols), bf16),
        compiler_params=pltpu.CompilerParams(vmem_limit_bytes=vmem_cap),
        cost_estimate=pl.CostEstimate(flops=0, bytes_accessed=cols, transcendentals=0),
        name="matrix_grad",
    )(left, right, *after)


def input_kernel(*refs, part, parts_n):
    weight_ref, pre_ref = refs[0], refs[1]
    out_ref, weight = refs[-2], refs[-1]
    shards = weight_ref.shape[0]

    @pl.when(pl.program_id(0) == 0)
    def _():
        for shard in range(shards):
            weight[shard * part : (shard + 1) * part, :] = weight_ref[shard, :part, :]

    grads = jnp.concatenate([ref[...] for ref in refs[2 : 2 + parts_n]], axis=1)
    out_ref[...] = (pre_ref[...] + dot(grads, weight[...], rows_by_rows)).astype(bf16)


def input_gradient(weight, grad_pre, parts, after):
    tokens, width = grad_pre.shape
    tile = min(512, tokens)

    def row(n):
        return pl.BlockSpec((tile, n), lambda i: (i, 0))

    return pl.pallas_call(
        functools.partial(input_kernel, part=width // weight.shape[0], parts_n=len(parts)),
        grid=(tokens // tile,),
        in_specs=[pl.BlockSpec(weight.shape, lambda i: (0, 0, 0), pipeline_mode=pl.Buffered(1))]
        + [row(width)]
        + [row(part.shape[1]) for part in parts]
        + [pl.BlockSpec(memory_space=pl.ANY)] * len(after),
        out_specs=row(width),
        out_shape=jax.ShapeDtypeStruct((tokens, width), bf16),
        scratch_shapes=[pltpu.VMEM((width, weight.shape[2]), bf16)],
        compiler_params=pltpu.CompilerParams(vmem_limit_bytes=vmem_cap),
        cost_estimate=pl.CostEstimate(flops=0, bytes_accessed=tokens, transcendentals=0),
        name="input_gradient",
    )(weight, grad_pre, *parts, *after)


def token_kernel(
    attended_ref,
    x_ref,
    cot_ref,
    weights_ref,
    vec_ref,
    bias_up_ref,
    out_ref,
    hidden_ref,
    active_ref,
    grad_mlp_ref,
    grad_upper_ref,
    grad_pre_ref,
    grad_branch_ref,
    grad_attended_ref,
    sums_ref,
    sums_up_ref,
    weight_out,
    weight_up,
    weight_down,
    slope,
    arrived,
):
    shards, part = weights_ref.shape[:2]
    width, hidden_n = weight_up.shape
    chunks = hidden_n // width

    copies = [[], [], []]
    for shard in range(shards):
        rows = pl.ds(shard * part, part)
        mine = weights_ref.at[shard]
        copies[0].append((mine.at[:, pl.ds(0, width)], weight_out.at[rows, :]))
        copies[1].append((mine.at[:, pl.ds(width, hidden_n)], weight_up.at[rows, :]))
        for chunk in range(chunks):
            start = width + hidden_n + chunk * width
            rows = pl.ds((shard * chunks + chunk) * part, part)
            copies[2].append((mine.at[:, pl.ds(start, width)], weight_down.at[rows, :]))
    starts = [0, shards, 2 * shards]
    copies = [
        [
            pltpu.make_async_copy(source, target, arrived.at[start + place])
            for place, (source, target) in enumerate(some)
        ]
        for start, some in zip(starts, copies)
    ]

    def wait_for(place):
        @pl.when(pl.program_id(0) == 0)
        def _():
            for copy in copies[place]:
                copy.wait()

    @pl.when(pl.program_id(0) == 0)
    def _():
        for some in copies:
            for copy in some:
                copy.start()
        sums_ref[...] = jnp.zeros_like(sums_ref)
        sums_up_ref[...] = jnp.zeros_like(sums_up_ref)

    bias_out, gain_one, shift_one, bias_down, gain_two, shift_two = [
        vec_ref[place : place + 1, :] for place in range(6)
    ]

    def mean(value):
        return jnp.mean(value, axis=1, keepdims=True)

    def add_to(place, value):
        sums_ref[place : place + 1, :] += jnp.sum(value.astype(f32), axis=0, keepdims=True)

    def normed(value):
        centred = value - mean(value)
        inverse = lax.rsqrt(mean(centred * centred) + eps_norm)
        return centred * inverse, inverse

    def norm_backward(incoming, normed_value, inverse, gain):
        scaled = incoming * gain
        centred = scaled - mean(scaled) - normed_value * mean(scaled * normed_value)
        return centred * inverse

    wait_for(0)
    branch = dot(attended_ref[...], weight_out[...]) + bias_out
    normed_one, inverse_one = normed(x_ref[...].astype(f32) + branch)
    hidden = normed_one * gain_one + shift_one
    hidden_low = hidden.astype(bf16)
    hidden_ref[...] = hidden_low
    mlp_out = jnp.zeros_like(hidden)
    wait_for(1)
    wait_for(2)
    for chunk in range(chunks):
        cols = slice(chunk * width, (chunk + 1) * width)
        upper = dot(hidden_low, weight_up[:, cols]) + bias_up_ref[:, cols]
        share = 0.5 * (1.0 + lax.erf(upper * 0.5**0.5))
        density = jnp.exp(-0.5 * upper * upper) * (2.0 * jnp.pi) ** -0.5
        active = (upper * share).astype(bf16)
        active_ref[:, cols] = active
        slope[:, cols] = share + upper * density
        mlp_out = mlp_out + dot(active, weight_down[cols, :])
    normed_two, inverse_two = normed(hidden + (mlp_out + bias_down))
    out_ref[...] = (normed_two * gain_two + shift_two).astype(bf16)

    incoming = cot_ref[...].astype(f32)
    grad_sum = norm_backward(incoming, normed_two, inverse_two, gain_two)
    grad_mlp = grad_sum.astype(bf16)
    grad_mlp_ref[...] = grad_mlp
    add_to(5, incoming)
    add_to(4, incoming * normed_two)
    add_to(3, grad_mlp)
    grad_hidden = grad_sum
    for chunk in range(chunks):
        cols = slice(chunk * width, (chunk + 1) * width)
        grad_active = dot(grad_mlp, weight_down[cols, :], rows_by_rows)
        grad_upper = (grad_active * slope[:, cols]).astype(bf16)
        grad_upper_ref[:, cols] = grad_upper
        sums_up_ref[0:1, cols] += jnp.sum(grad_upper.astype(f32), axis=0, keepdims=True)
        grad_hidden = grad_hidden + dot(grad_upper, weight_up[:, cols], rows_by_rows)
    grad_pre = norm_backward(grad_hidden, normed_one, inverse_one, gain_one)
    grad_pre_ref[...] = grad_pre
    grad_branch = grad_pre.astype(bf16)
    grad_branch_ref[...] = grad_branch
    add_to(2, grad_hidden)
    add_to(1, grad_hidden * normed_one)
    add_to(0, grad_branch)
    grad_attended_ref[...] = dot(grad_branch, weight_out[...], rows_by_rows).astype(bf16)


def token_parts(attended, x, cotangent, weights, vecs, bias_up):
    tokens, width = x.shape
    shards, part, cols = weights.shape
    hidden_n = (cols - width) // 2
    tile = 256

    def row(n):
        return pl.BlockSpec((tile, n), lambda i: (i, 0))

    def fixed(shape):
        return pl.BlockSpec(shape, lambda i: (0, 0))

    def shape(n, kind=bf16):
        return jax.ShapeDtypeStruct((tokens, n), kind)

    copies = shards * (2 + hidden_n // width)
    return pl.pallas_call(
        token_kernel,
        grid=(tokens // tile,),
        in_specs=[row(width)] * 3
        + [pl.BlockSpec(memory_space=pl.ANY), fixed(vecs.shape), fixed(bias_up.shape)],
        out_specs=[
            row(width),
            row(width),
            row(hidden_n),
            row(width),
            row(hidden_n),
            row(width),
            row(width),
            row(width),
            fixed((8, width)),
            fixed((8, hidden_n)),
        ],
        out_shape=[
            shape(width),
            shape(width),
            shape(hidden_n),
            shape(width),
            shape(hidden_n),
            shape(width, f32),
            shape(width),
            shape(width),
            jax.ShapeDtypeStruct((8, width), f32),
            jax.ShapeDtypeStruct((8, hidden_n), f32),
        ],
        scratch_shapes=[
            pltpu.VMEM((width, width), bf16),
            pltpu.VMEM((width, hidden_n), bf16),
            pltpu.VMEM((hidden_n, width), bf16),
            pltpu.VMEM((tile, hidden_n), f32),
            pltpu.SemaphoreType.DMA((copies,)),
        ],
        compiler_params=pltpu.CompilerParams(vmem_limit_bytes=vmem_cap),
        cost_estimate=pl.CostEstimate(flops=0, bytes_accessed=tokens, transcendentals=0),
        name="token_parts",
    )(attended, x, cotangent, weights, vecs, bias_up)


def body(
    inputs,
    segments,
    random_blocks,
    cotangent,
    qkv_weight,
    qv_bias,
    out_weight,
    out_bias,
    norm1_gain,
    norm1_bias,
    up_weight,
    up_bias,
    down_weight,
    down_bias,
    norm2_gain,
    norm2_bias,
):
    seq_count, run, width = inputs.shape
    per_dev, head_count, rand_count = random_blocks.shape[1:]
    block = run // per_dev
    head_size = width // head_count
    dp_count = lax.axis_size("dp")
    ctx_count = lax.axis_size("ctx")
    ctx_index = lax.axis_index("ctx")
    team = ctx_count // seq_count
    tokens = seq_count * run

    x = swap_pieces(inputs, "ctx", team).reshape(tokens, width)
    lists = swap_pieces(tied(random_blocks.reshape(seq_count, 1, -1), x), "ctx", team)

    def back_to_runs(rows):
        return swap_pieces(rows.reshape(seq_count, run, width), "ctx", team)

    vectors = (qv_bias, out_bias, norm1_gain, norm1_bias, up_bias, down_bias, norm2_gain, norm2_bias)
    sizes = [v.shape[0] for v in vectors]
    qkv_rows, qkv_cols = qkv_weight.shape
    first = lax.all_gather(pack_weights(qkv_weight, vectors), "dp", axis=0)
    others = lax.all_gather(join_weights(out_weight, up_weight, down_weight), "dp", axis=0)

    def vector(place):
        return first[:, qkv_rows + place, : sizes[place]].reshape(1, -1).astype(f32)

    bias_qv, bias_up = vector(0), vector(4)
    vecs = first[:, qkv_rows + 1 : qkv_rows + 8, :qkv_rows].transpose(1, 0, 2).reshape(7, width)
    vecs = jnp.concatenate([vecs[:3], vecs[4:], jnp.zeros_like(vecs[:2])], axis=0).astype(f32)

    seq_index = ctx_index // team
    seg = lax.dynamic_index_in_dim(segments, seq_index, 0, keepdims=False)
    lists = lists.reshape(seq_count, per_dev, head_count, rand_count)
    if team > 1:
        team_index = ctx_index % team
        held = -(-head_count // (2 * team)) * 2
        spare = held * team - head_count
        lists = share_pieces(lists, "ctx", team).transpose(1, 0, 2, 3, 4)
        lists = jnp.pad(lists.reshape(-1, head_count, rand_count), ((0, 0), (0, spare), (0, 0)))
        lists = lax.dynamic_slice_in_dim(lists, team_index * held, held, 1)
    else:
        lists = lists.reshape(-1, head_count, rand_count)
    features = mask_features(seg, lists, block)

    def to_heads(rows):
        if team == 1:
            return rows
        rows = jnp.pad(rows, ((0, 0), (0, spare * head_size)))
        part = swap_pieces(rows.reshape(tokens, team, -1).transpose(1, 0, 2), "ctx", 1)
        part = part.reshape(team, seq_count, run, -1).transpose(1, 0, 2, 3)
        return part.reshape(team * tokens, -1)

    def to_tokens(part):
        if team == 1:
            return part
        part = part.reshape(seq_count, team, run, -1).transpose(1, 0, 2, 3)
        rows = swap_pieces(part.reshape(team, tokens, -1), "ctx", 1)
        return rows.transpose(1, 0, 2).reshape(tokens, -1)[:, :width]

    queries, keys, values = project(x, first, bias_qv)
    grad_result = swap_pieces(copied(cotangent, x), "ctx", team).reshape(tokens, width)
    heads = tuple(to_heads(part) for part in (queries, keys, values))
    attended = attend(forward_kernel, heads, features, 1, head_size, "attend_forward")[0]
    attended = to_tokens(attended)
    parts = token_parts(attended, x, grad_result, others, vecs, bias_up)
    result, hidden_low, active, grad_mlp, grad_upper, grad_pre, grad_branch, grad_att, sums, sums_up = parts

    down_grad = matrix_grad(active, grad_mlp)
    down_part = scattered(down_grad)
    place = lax.axis_index("dp").reshape(1).astype(jnp.int32)
    up = Scatter(*wide_grad(place, hidden_low, grad_upper, dp_count, (down_grad,)))
    sent = up.begin()
    layer_out = back_to_runs(tied(result, sent))
    up.end()
    sent = up.begin(sent)
    back_heads = heads + (to_heads(grad_att),)
    pair_count = back_heads[0].shape[1] // lanes_n
    back = attend(backward_kernel, back_heads, features, 3, head_size, "attend_backward", (sent,))
    if team > 1:
        back = [to_tokens(array) for array in back[:3]]
        back.append(jnp.stack([jnp.sum(back[i].astype(f32), axis=0) for i in (0, 2)]))
    *back, bias_sums = back
    def shard_rows(values):
        return values.reshape(dp_count, -1, qkv_rows).transpose(1, 0, 2).reshape(-1, width)

    side = [shard_rows(bias_sums[:2].reshape(-1)), sums[:6], shard_rows(sums_up[0])]
    side_rows = [part.shape[0] for part in side]
    side_n = -(-sum(side_rows) // lanes_n) * lanes_n
    side.append(jnp.zeros((side_n - sum(side_rows), width), f32))
    wide = Chain([[down_part], up.end(back[0])])
    sent = wide.begin(back[0])
    groups = [(attended, [grad_branch]), (x, back)]
    grads = weight_grads(
        place, groups, jnp.concatenate(side, axis=0), dp_count, (sent, layer_out)
    )
    rest = Scatter(*grads)
    sent = rest.begin()
    result = input_gradient(first, grad_pre, back, (sent,))
    input_grad = back_to_runs(tied(result, sent))
    rest.end(result)
    sent = rest.begin()
    sent = wide.next(sent)
    rest_bits = (ctx_count - 1).bit_length()
    rest = Chain([rest.end(sent)])
    sent = rest.begin(sent)
    while len(wide.plan) > rest_bits + 1:
        sent = wide.next(sent)
    sent = rest.next(sent)
    wide.end(sent)
    pieces = added(wide.parts[0])
    rest.next(pieces, input_grad)
    pieces = lax.all_gather(pieces, "ctx", axis=0)
    while len(rest.plan) > 1:
        rest.next()
    rest.end()
    bits = rest_bits
    pieces = pieces.reshape((2,) * bits + pieces.shape[1:])
    pieces = pieces.transpose(tuple(reversed(range(bits))) + (bits, bits + 1))
    pieces = pieces.reshape(-1, 2 * width).astype(f32)
    down_total = pieces[:, :width]
    up_total = pieces[:, width:].reshape(-1, qkv_rows, width).transpose(1, 0, 2)
    up_total = up_total.reshape(qkv_rows, -1)
    total = rest.parts[0][0].astype(f32)
    out_total, qkv_total = total[:, :width], total[:, width : width + qkv_cols]
    flat = total[:, width + qkv_cols : width + qkv_cols + sum(side_rows)].T
    starts = [0, 2, 3, 4, 8, 5, 6, 7]
    vec_totals = [
        flat[start : start + size // qkv_rows].reshape(-1) for start, size in zip(starts, sizes)
    ]
    return (
        layer_out,
        input_grad,
        qkv_total,
        vec_totals[0],
        out_total,
        vec_totals[1],
        vec_totals[2],
        vec_totals[3],
        up_total,
        vec_totals[4],
        down_total,
        vec_totals[5],
        vec_totals[6],
        vec_totals[7],
    )


def solution(mesh):
    tokens = P("dp", "ctx", None)
    matrix, vector = P("dp", None), P("dp")
    weights = (matrix, vector, matrix, vector, vector, vector, matrix, vector, matrix, vector, vector, vector)
    return jax.shard_map(
        body,
        mesh=mesh,
        in_specs=(tokens, matrix, P("dp", "ctx", None, None), tokens) + weights,
        out_specs=(tokens, tokens) + weights,
        check_vma=False,
    )
```

```python
import functools
import math

import jax
import jax.numpy as jnp
from jax import lax
from jax.experimental import pallas as pl
from jax.experimental.pallas import tpu as pltpu
from jax.sharding import PartitionSpec as P

f32, bf16 = jnp.float32, jnp.bfloat16
eps_norm = 1e-12
far = 1e30
doc_min = 200
lanes_n = 128
vmem_cap = 56 * 2**20


def swap_pieces(pieces, axis, stride):
    count, size = pieces.shape[0], lax.axis_size(axis)
    groups = None
    if count < size:
        span = stride * count
        starts = [base + offset for base in range(0, size, span) for offset in range(stride)]
        groups = [[start + i * stride for i in range(count)] for start in starts]
    return lax.all_to_all(pieces, axis, 0, 0, axis_index_groups=groups, tiled=True)


def share_pieces(piece, axis, count):
    size = lax.axis_size(axis)
    member = lax.axis_index(axis) % count
    came, stride = piece[None], 1
    while stride < count:
        other = lax.ppermute(came, axis, [(i, i ^ stride) for i in range(size)])
        upper = (member // stride) % 2 == 1
        came = jnp.concatenate([jnp.where(upper, other, came), jnp.where(upper, came, other)], axis=0)
        stride *= 2
    return came


def tied(value, *deps):
    def nothing(*refs):
        pass

    return pl.pallas_call(
        nothing,
        in_specs=[pl.BlockSpec(memory_space=pl.ANY)] * (1 + len(deps)),
        out_specs=pl.BlockSpec(memory_space=pl.ANY),
        out_shape=jax.ShapeDtypeStruct(value.shape, value.dtype),
        input_output_aliases={0: 0},
        name="tied",
    )(value, *deps)


def added(terms):
    if len(terms) == 1:
        return terms[0]
    total = terms[0].astype(f32)
    for term in terms[1:]:
        total = total + term.astype(f32)
    return total.astype(bf16)


class Chain:
    def __init__(self, parts, axis="ctx"):
        self.parts = parts
        strides, stride = [], 1
        while stride < lax.axis_size(axis):
            strides.append(stride)
            stride *= 2
        self.axis = axis
        self.plan = [(stride, True) for stride in strides]
        if axis == "ctx":
            self.plan += [(stride, False) for stride in reversed(strides)]

    def halves(self, stride):
        member = (lax.axis_index(self.axis) // stride) % 2

        def half(which):
            columns = []
            for terms in self.parts:
                rows = terms[0].shape[0] // 2
                cut = [lax.dynamic_slice_in_dim(term, which * rows, rows, 0) for term in terms]
                columns.append(added(cut))
            return columns[0] if len(columns) == 1 else jnp.concatenate(columns, axis=1)

        return half(member), half(1 - member)

    def begin(self, *after):
        stride, adds = self.plan[0]
        if adds:
            self.kept, sent = self.halves(stride)
            sent = tied(sent, *after)
        else:
            sent = tied(added(self.parts[0]), *after)
            self.kept = sent
        size = lax.axis_size(self.axis)
        self.came = lax.ppermute(sent, self.axis, [(i, i ^ stride) for i in range(size)])
        return sent

    def end(self, *after):
        stride, adds = self.plan.pop(0)
        came = tied(self.came, *after) if after else self.came
        if adds:
            self.parts = [[self.kept, came]]
        else:
            upper = (lax.axis_index(self.axis) // stride) % 2 == 1
            pair = [jnp.where(upper, came, self.kept), jnp.where(upper, self.kept, came)]
            self.parts = [[jnp.concatenate(pair, axis=0)]]
        return self.parts[0]

    def next(self, *after):
        self.end()
        return self.begin(*after)

    def open(self):
        return len(self.plan) > 0


class Scatter:
    def __init__(self, kept, sent):
        self.kept, self.came, self.stride = kept, None, 1
        self.sent = sent

    def begin(self, *after):
        size = lax.axis_size("dp")
        sent = tied(self.sent, *after)
        self.came = lax.ppermute(sent, "dp", [(i, i ^ self.stride) for i in range(size)])
        return sent

    def end(self, *after):
        came = tied(self.came, *after) if after else self.came
        self.stride *= 2
        if self.stride == lax.axis_size("dp"):
            return [self.kept, came]
        rows = self.kept.shape[0] // 2
        self.sent = added([self.kept[rows:], came[rows:]])
        self.kept = added([self.kept[:rows], came[:rows]])
        return None


def copied(value, *deps):
    def copy(value_ref, *refs):
        refs[-1][...] = value_ref[...]

    return pl.pallas_call(
        copy,
        in_specs=[pl.BlockSpec(memory_space=pltpu.VMEM)]
        + [pl.BlockSpec(memory_space=pl.ANY)] * len(deps),
        out_shape=jax.ShapeDtypeStruct(value.shape, value.dtype),
        name="copied",
    )(value, *deps)


def scattered(grad):
    return lax.psum_scatter(grad, "dp", scatter_dimension=0, tiled=True)


def mask_features(seg, rand, block):
    tokens = seg.shape[0]
    blocks, heads = rand.shape[:2]
    seg_limit = tokens // doc_min + 1
    used = seg_limit + 2 * blocks
    width = -(-used // lanes_n) * lanes_n
    ids = jnp.arange(blocks, dtype=jnp.int32)

    def hot(values):
        return (values[..., None] == ids).astype(jnp.int32)

    near = hot(ids - 1) + hot(ids) + hot(ids + 1) + hot(ids * 0) + hot(ids * 0 + blocks - 1)
    counts = near[:, None, :] + jnp.sum(hot(rand), axis=2)
    edge = (ids == 0) | (ids == blocks - 1)
    counts = jnp.where(edge[:, None, None], 1, counts).transpose(1, 2, 0)
    log_count = jnp.log(jnp.maximum(counts, 1).astype(f32))
    high = log_count.astype(bf16).astype(f32)
    low = jnp.where(counts > 0, log_count - high, 0.0)
    high = jnp.where(counts > 0, high, -far)
    table = jnp.concatenate(
        [
            jnp.zeros((heads, blocks, seg_limit), f32),
            high,
            low,
            jnp.zeros((heads, blocks, width - used), f32),
        ],
        axis=2,
    )
    lane = jnp.arange(width, dtype=jnp.int32)[None]
    own = (jnp.arange(tokens, dtype=jnp.int32) // block)[:, None]
    is_seg = lane < seg_limit
    same = lane == seg[:, None]
    key_feat = jnp.where(is_seg & same, 1.0, 0.0).astype(bf16)
    own_lane = (lane - seg_limit == own) | (lane - seg_limit - blocks == own)
    query_feat = jnp.where(
        is_seg, jnp.where(same, 0.0, -far), jnp.where(own_lane, 1.0, 0.0)
    ).astype(bf16)
    near = -(-seg_limit // lanes_n) * lanes_n
    return key_feat[:, :near], query_feat[:, :near], table


def fill_keys(k_ref, key_feat_ref, table_ref, keys):
    tokens, near = key_feat_ref.shape
    blocks, width = table_ref.shape[1:]
    feat = key_feat_ref[...].astype(f32).reshape(blocks, tokens // blocks, near)
    for side in range(2):
        rows = table_ref[side][:, None, :]
        both = (feat + rows[..., :near]).reshape(tokens, near)
        keys[side, :, :lanes_n] = k_ref[...]
        keys[side, :, lanes_n : lanes_n + near] = both.astype(bf16)
        if width > near:
            rest = jnp.broadcast_to(rows[..., near:], (blocks, tokens // blocks, width - near))
            keys[side, :, lanes_n + near :] = rest.reshape(tokens, width - near).astype(bf16)


def query_lanes(near_feat, start, tokens, blocks, width):
    rows, near = near_feat.shape
    if width == near:
        return near_feat
    shape = (rows, width - near)
    lane = lax.broadcasted_iota(jnp.int32, shape, 1) + near - (tokens // doc_min + 1)
    own = (lax.broadcasted_iota(jnp.int32, shape, 0) + start) // (tokens // blocks)
    rest = jnp.where((lane == own) | (lane - blocks == own), 1.0, 0.0).astype(bf16)
    return jnp.concatenate([near_feat, rest], axis=1)


rows_by_rows = (((1,), (1,)), ((), ()))
cols_by_cols = (((0,), (0,)), ((), ()))


def dot(left, right, dims=(((1,), (0,)), ((), ()))):
    return lax.dot_general(left, right, dims, preferred_element_type=f32)


def forward_kernel(
    q_ref, k_ref, v_ref, key_feat_ref, query_feat_ref, table_ref, out_ref, keys, vals, *, half, tile
):
    tokens = q_ref.shape[0]
    fill_keys(k_ref, key_feat_ref, table_ref, keys)
    vals[:, :lanes_n] = v_ref[...]
    vals[:, lanes_n:] = jnp.ones((tokens, lanes_n), bf16)

    @pl.loop(0, tokens // tile)
    def _(step):
        rows = pl.ds(pl.multiple_of(step * tile, tile), tile)
        q = q_ref[rows, :] * bf16(half**-0.5)
        side_of = lax.broadcasted_iota(jnp.int32, (tile, lanes_n), 1) // half
        feat = query_lanes(query_feat_ref[rows, :], step * tile, tokens, *table_ref.shape[1:])
        scores = [
            dot(
                jnp.concatenate([jnp.where(side_of == side, q, bf16(0)), feat], axis=1),
                keys[side],
                rows_by_rows,
            )
            for side in range(2)
        ]
        outs = []
        for score in scores:
            weights = jnp.exp(score - jnp.max(score, axis=1, keepdims=True)).astype(bf16)
            mixed = dot(weights, vals[...])
            outs.append(mixed[:, :lanes_n] / mixed[:, lanes_n:])
        out_ref[rows, :] = jnp.where(side_of == 0, outs[0], outs[1]).astype(bf16)


def backward_kernel(
    q_ref,
    k_ref,
    v_ref,
    grad_ref,
    key_feat_ref,
    query_feat_ref,
    table_ref,
    dq_ref,
    dk_ref,
    dv_ref,
    sums_ref,
    keys,
    dk_sum,
    dv_sum,
    *,
    half,
    tile,
):
    tokens = q_ref.shape[0]
    fill_keys(k_ref, key_feat_ref, table_ref, keys)
    dk_sum[...] = jnp.zeros_like(dk_sum)
    dv_sum[...] = jnp.zeros_like(dv_sum)
    sums_ref[...] = jnp.zeros_like(sums_ref)

    @pl.loop(0, tokens // tile)
    def _(step):
        rows = pl.ds(pl.multiple_of(step * tile, tile), tile)
        q_pair = q_ref[rows, :] * bf16(half**-0.5)
        grad_pair = grad_ref[rows, :]
        side_of = lax.broadcasted_iota(jnp.int32, (tile, lanes_n), 1) // half
        feat = query_lanes(query_feat_ref[rows, :], step * tile, tokens, *table_ref.shape[1:])
        queries = [jnp.where(side_of == side, q_pair, bf16(0)) for side in range(2)]
        grads = [jnp.where(side_of == side, grad_pair, bf16(0)) for side in range(2)]
        probs, dscores = [], []
        for side in range(2):
            wide = jnp.concatenate([queries[side], feat], axis=1)
            scores = dot(wide, keys[side], rows_by_rows)
            dprobs = dot(grads[side], v_ref[...], rows_by_rows)
            raw = jnp.exp(scores - jnp.max(scores, axis=1, keepdims=True))
            prob = raw * (1.0 / jnp.sum(raw, axis=1, keepdims=True))
            both = prob * dprobs
            dscore = both - prob * jnp.sum(both, axis=1, keepdims=True)
            probs.append(prob.astype(bf16))
            dscores.append(dscore.astype(bf16))
        dv_sum[...] += dot(
            jnp.concatenate(probs, axis=0), jnp.concatenate(grads, axis=0), cols_by_cols
        )
        dk_sum[...] += dot(
            jnp.concatenate(dscores, axis=0), jnp.concatenate(queries, axis=0), cols_by_cols
        )
        dqs = [dot(dscore, k_ref[...]) for dscore in dscores]
        dq = (jnp.where(side_of == 0, dqs[0], dqs[1]) * half**-0.5).astype(bf16)
        dq_ref[rows, :] = dq
        sums_ref[0:1, :] += jnp.sum(dq.astype(f32), axis=0, keepdims=True)

    dk_ref[...] = dk_sum[...].astype(bf16)
    dv = dv_sum[...].astype(bf16)
    dv_ref[...] = dv
    sums_ref[1:2, :] = jnp.sum(dv.astype(f32), axis=0, keepdims=True)


def attend(kernel, arrays, features, outs, half, name, after=(), first=0, count=None):
    tokens, width = arrays[0].shape
    key_feat, query_feat, table = features
    count = width // lanes_n if count is None else count
    near, feat_width = key_feat.shape[1], table.shape[2]
    tile = tokens if tokens <= 1024 else 32
    once = {"pipeline_mode": pl.Buffered(1)} if count == 1 else {}
    pair = pl.BlockSpec((tokens, lanes_n), lambda p: (0, p + first), **once)
    pair_out = pl.BlockSpec((tokens, lanes_n), lambda p: (0, p), **once)
    whole = pl.BlockSpec((tokens, near), lambda p: (0, 0), pipeline_mode=pl.Buffered(1))
    shape = jax.ShapeDtypeStruct((tokens, count * lanes_n), bf16)
    scratch = [pltpu.VMEM((2, tokens, lanes_n + feat_width), bf16)]
    if outs == 1:
        scratch = scratch + [pltpu.VMEM((tokens, 2 * lanes_n), bf16)]
    else:
        scratch = scratch + [pltpu.VMEM((tokens, lanes_n), f32)] * 2

    def run(*refs):
        held = len(arrays) + 3
        kernel(*refs[:held], *refs[held + len(after) :], half=half, tile=tile)

    return pl.pallas_call(
        run,
        grid=(count,),
        in_specs=[pair] * len(arrays)
        + [whole, whole]
        + [pl.BlockSpec((2,) + table.shape[1:], lambda p: (p + first, 0, 0))]
        + [pl.BlockSpec(memory_space=pl.ANY)] * len(after),
        out_specs=[pair_out] * outs + [pl.BlockSpec((8, lanes_n), lambda p: (0, p))] * (outs > 1),
        out_shape=[shape] * outs
        + [jax.ShapeDtypeStruct((8, count * lanes_n), f32)] * (outs > 1),
        scratch_shapes=scratch,
        compiler_params=pltpu.CompilerParams(vmem_limit_bytes=vmem_cap),
        cost_estimate=pl.CostEstimate(flops=0, bytes_accessed=tokens, transcendentals=0),
        name=name,
    )(*arrays, key_feat, query_feat, table, *after)


def pack_kernel(weight_ref, *refs):
    out_ref = refs[-1]
    rows = weight_ref.shape[0]
    out_ref[:rows, :] = weight_ref[...]
    out_ref[rows:, :] = jnp.zeros_like(out_ref[rows:, :])
    for place, ref in enumerate(refs[:-1]):
        out_ref[rows + place : rows + place + 1, : ref.shape[0]] = ref[...].reshape(1, -1)


def pack_weights(weight, vectors):
    rows, cols = weight.shape
    extra = -(-len(vectors) // 16) * 16
    return pl.pallas_call(
        pack_kernel,
        out_shape=jax.ShapeDtypeStruct((rows + extra, cols), weight.dtype),
        name="pack_weights",
    )(weight, *vectors)


def join_kernel(out_ref, up_ref, down_ref, all_ref):
    rows, width = out_ref.shape
    hidden_n = up_ref.shape[1]
    all_ref[:, :width] = out_ref[...]
    all_ref[:, width : width + hidden_n] = up_ref[...]
    for part in range(hidden_n // width):
        start = width + hidden_n + part * width
        all_ref[:, start : start + width] = down_ref[part * rows : (part + 1) * rows, :]


def join_weights(out_weight, up_weight, down_weight):
    rows, width = out_weight.shape
    return pl.pallas_call(
        join_kernel,
        out_shape=jax.ShapeDtypeStruct((rows, width + 2 * up_weight.shape[1]), out_weight.dtype),
        compiler_params=pltpu.CompilerParams(vmem_limit_bytes=vmem_cap),
        name="join_weights",
    )(out_weight, up_weight, down_weight)


def project_kernel(x_ref, weight_ref, bias_ref, q_ref, k_ref, v_ref, weight, *, part):
    shards = weight_ref.shape[0]
    width = x_ref.shape[1]

    @pl.when(pl.program_id(0) == 0)
    def _():
        for shard in range(shards):
            weight[shard * part : (shard + 1) * part, :] = weight_ref[shard, :part, :]

    x = x_ref[...]
    q_ref[...] = (dot(x, weight[:, :width]) + bias_ref[:, :width]).astype(bf16)
    k_ref[...] = dot(x, weight[:, width : 2 * width]).astype(bf16)
    v_ref[...] = (dot(x, weight[:, 2 * width :]) + bias_ref[:, width:]).astype(bf16)


def project(x, weight, bias):
    tokens, width = x.shape
    tile = min(512, tokens)
    row = pl.BlockSpec((tile, width), lambda i: (i, 0))
    shape = jax.ShapeDtypeStruct((tokens, width), bf16)
    return pl.pallas_call(
        functools.partial(project_kernel, part=width // weight.shape[0]),
        grid=(tokens // tile,),
        in_specs=[
            row,
            pl.BlockSpec(weight.shape, lambda i: (0, 0, 0), pipeline_mode=pl.Buffered(1)),
            pl.BlockSpec(bias.shape, lambda i: (0, 0)),
        ],
        out_specs=[row] * 3,
        out_shape=[shape] * 3,
        scratch_shapes=[pltpu.VMEM((width, weight.shape[2]), bf16)],
        compiler_params=pltpu.CompilerParams(vmem_limit_bytes=vmem_cap),
        cost_estimate=pl.CostEstimate(flops=0, bytes_accessed=tokens, transcendentals=0),
        name="project",
    )(x, weight, bias)


def sort_shards(place_ref, grad, kept_ref, sent_ref, shards, block, block_n):
    rows = grad.shape[0] // shards
    for shard in range(shards):
        turn = place_ref[0] ^ shard
        start = pl.multiple_of(((turn // 2) * block_n + block) * rows, rows)
        piece = grad[shard * rows : (shard + 1) * rows].astype(bf16)

        @pl.when(turn % 2 == 0)
        def _():
            kept_ref[pl.ds(start, rows), : grad.shape[1]] = piece

        @pl.when(turn % 2 == 1)
        def _():
            sent_ref[pl.ds(start, rows), : grad.shape[1]] = piece


def grads_kernel(place_ref, *refs, groups, held, shards):
    kept_ref, sent_ref = refs[-2:]
    grads = []
    for left, rights in groups:
        right = [refs[place][...] for place in rights]
        right = right[0] if len(right) == 1 else jnp.concatenate(right, axis=1)
        grads.append(dot(refs[left][...], right, cols_by_cols).astype(bf16))
    grads.append(jnp.transpose(refs[held - 1][...]).astype(bf16))
    sort_shards(place_ref, jnp.concatenate(grads, axis=1), kept_ref, sent_ref, shards, 0, 1)


def weight_grads(place, groups, extra, shards, after=()):
    arrays, places = [], []
    for left, rights in groups:
        places.append((len(arrays), tuple(range(len(arrays) + 1, len(arrays) + 1 + len(rights)))))
        arrays += [left] + list(rights)
    arrays.append(extra)
    cols = sum(right.shape[1] for _, rights in groups for right in rights) + extra.shape[0]
    held = len(arrays)
    half = jax.ShapeDtypeStruct((groups[0][0].shape[1] // 2, cols), bf16)
    return pl.pallas_call(
        functools.partial(grads_kernel, groups=places, held=held, shards=shards),
        in_specs=[pl.BlockSpec(memory_space=pltpu.SMEM)]
        + [pl.BlockSpec(memory_space=pltpu.VMEM)] * held
        + [pl.BlockSpec(memory_space=pl.ANY)] * len(after),
        out_shape=[half] * 2,
        compiler_params=pltpu.CompilerParams(vmem_limit_bytes=vmem_cap),
        cost_estimate=pl.CostEstimate(flops=0, bytes_accessed=cols, transcendentals=0),
        name="weight_grads",
    )(place, *arrays, *after)


def wide_grad_kernel(place_ref, left_ref, right_ref, *refs, shards):
    grad = dot(left_ref[...], right_ref[...], cols_by_cols)
    sort_shards(
        place_ref, grad, refs[-2], refs[-1], shards, pl.program_id(0), pl.num_programs(0)
    )


def wide_grad(place, left, right, shards, after=()):
    tokens, rows = left.shape
    runs = right.shape[1] // rows
    half = (rows * runs // 2, rows)
    whole = pl.BlockSpec(half, lambda i: (0, 0))
    return pl.pallas_call(
        functools.partial(wide_grad_kernel, shards=shards),
        grid=(runs,),
        in_specs=[
            pl.BlockSpec(memory_space=pltpu.SMEM),
            pl.BlockSpec((tokens, rows), lambda i: (0, 0)),
            pl.BlockSpec((tokens, rows), lambda i: (0, i)),
        ]
        + [pl.BlockSpec(memory_space=pl.ANY)] * len(after),
        out_specs=[whole] * 2,
        out_shape=[jax.ShapeDtypeStruct(half, bf16)] * 2,
        compiler_params=pltpu.CompilerParams(vmem_limit_bytes=vmem_cap),
        cost_estimate=pl.CostEstimate(flops=0, bytes_accessed=rows, transcendentals=0),
        name="wide_grad",
    )(place, left, right, *after)


def matrix_grad_kernel(left_ref, right_ref, *refs):
    refs[-1][...] = dot(left_ref[...], right_ref[...], cols_by_cols).astype(bf16)


def matrix_grad(left, right, after=()):
    tokens, rows = left.shape
    cols = right.shape[1]
    run = min(rows, cols)
    tall = rows > cols

    def taken(yes):
        return pl.BlockSpec((tokens, run), (lambda i: (0, i)) if yes else (lambda i: (0, 0)))

    return pl.pallas_call(
        matrix_grad_kernel,
        grid=(max(rows, cols) // run,),
        in_specs=[taken(tall), taken(not tall)] + [pl.BlockSpec(memory_space=pl.ANY)] * len(after),
        out_specs=pl.BlockSpec((run, run), (lambda i: (i, 0)) if tall else (lambda i: (0, i))),
        out_shape=jax.ShapeDtypeStruct((rows, cols), bf16),
        compiler_params=pltpu.CompilerParams(vmem_limit_bytes=vmem_cap),
        cost_estimate=pl.CostEstimate(flops=0, bytes_accessed=cols, transcendentals=0),
        name="matrix_grad",
    )(left, right, *after)


def spread_kernel(pieces_ref, down_ref, up_ref):
    count, rows, cols = pieces_ref.shape
    width = cols // 2
    part = up_ref.shape[0]
    bits = (count - 1).bit_length()
    for device in range(count):
        place = sum(((device >> bit) & 1) << (bits - 1 - bit) for bit in range(bits))
        piece = pieces_ref[device].astype(f32)
        down_ref[place * rows : (place + 1) * rows, :] = piece[:, :width]
        for start in range(0, rows, math.gcd(rows, part)):
            size = math.gcd(rows, part)
            run, row = divmod(place * rows + start, part)
            cells = piece[start : start + size, width:]
            up_ref[row : row + size, run * width : (run + 1) * width] = cells


def spread_gradients(pieces, part):
    count, rows, cols = pieces.shape
    width = cols // 2
    return pl.pallas_call(
        spread_kernel,
        out_shape=[
            jax.ShapeDtypeStruct((count * rows, width), f32),
            jax.ShapeDtypeStruct((part, count * rows // part * width), f32),
        ],
        compiler_params=pltpu.CompilerParams(vmem_limit_bytes=vmem_cap),
        name="spread_gradients",
    )(pieces)


def input_kernel(*refs, part, parts_n):
    weight_ref, pre_ref = refs[0], refs[1]
    out_ref, weight = refs[-2], refs[-1]
    shards = weight_ref.shape[0]

    @pl.when(pl.program_id(0) == 0)
    def _():
        for shard in range(shards):
            weight[shard * part : (shard + 1) * part, :] = weight_ref[shard, :part, :]

    grads = jnp.concatenate([ref[...] for ref in refs[2 : 2 + parts_n]], axis=1)
    out_ref[...] = (pre_ref[...] + dot(grads, weight[...], rows_by_rows)).astype(bf16)


def input_gradient(weight, grad_pre, parts, after):
    tokens, width = grad_pre.shape
    tile = min(512, tokens)

    def row(n):
        return pl.BlockSpec((tile, n), lambda i: (i, 0))

    return pl.pallas_call(
        functools.partial(input_kernel, part=width // weight.shape[0], parts_n=len(parts)),
        grid=(tokens // tile,),
        in_specs=[pl.BlockSpec(weight.shape, lambda i: (0, 0, 0), pipeline_mode=pl.Buffered(1))]
        + [row(width)]
        + [row(part.shape[1]) for part in parts]
        + [pl.BlockSpec(memory_space=pl.ANY)] * len(after),
        out_specs=row(width),
        out_shape=jax.ShapeDtypeStruct((tokens, width), bf16),
        scratch_shapes=[pltpu.VMEM((width, weight.shape[2]), bf16)],
        compiler_params=pltpu.CompilerParams(vmem_limit_bytes=vmem_cap),
        cost_estimate=pl.CostEstimate(flops=0, bytes_accessed=tokens, transcendentals=0),
        name="input_gradient",
    )(weight, grad_pre, *parts, *after)


def token_kernel(
    attended_ref,
    x_ref,
    cot_ref,
    weights_ref,
    vec_ref,
    bias_up_ref,
    out_ref,
    hidden_ref,
    active_ref,
    grad_mlp_ref,
    grad_upper_ref,
    grad_pre_ref,
    grad_branch_ref,
    grad_attended_ref,
    sums_ref,
    sums_up_ref,
    weight_out,
    weight_up,
    weight_down,
    slope,
    arrived,
):
    shards, part = weights_ref.shape[:2]
    width, hidden_n = weight_up.shape
    chunks = hidden_n // width

    copies = [[], [], []]
    for shard in range(shards):
        rows = pl.ds(shard * part, part)
        mine = weights_ref.at[shard]
        copies[0].append((mine.at[:, pl.ds(0, width)], weight_out.at[rows, :]))
        copies[1].append((mine.at[:, pl.ds(width, hidden_n)], weight_up.at[rows, :]))
        for chunk in range(chunks):
            start = width + hidden_n + chunk * width
            rows = pl.ds((shard * chunks + chunk) * part, part)
            copies[2].append((mine.at[:, pl.ds(start, width)], weight_down.at[rows, :]))
    starts = [0, shards, 2 * shards]
    copies = [
        [
            pltpu.make_async_copy(source, target, arrived.at[start + place])
            for place, (source, target) in enumerate(some)
        ]
        for start, some in zip(starts, copies)
    ]

    def wait_for(place):
        @pl.when(pl.program_id(0) == 0)
        def _():
            for copy in copies[place]:
                copy.wait()

    @pl.when(pl.program_id(0) == 0)
    def _():
        for some in copies:
            for copy in some:
                copy.start()
        sums_ref[...] = jnp.zeros_like(sums_ref)
        sums_up_ref[...] = jnp.zeros_like(sums_up_ref)

    bias_out, gain_one, shift_one, bias_down, gain_two, shift_two = [
        vec_ref[place : place + 1, :] for place in range(6)
    ]

    def mean(value):
        return jnp.mean(value, axis=1, keepdims=True)

    def add_to(place, value):
        sums_ref[place : place + 1, :] += jnp.sum(value.astype(f32), axis=0, keepdims=True)

    def normed(value):
        centred = value - mean(value)
        inverse = lax.rsqrt(mean(centred * centred) + eps_norm)
        return centred * inverse, inverse

    def norm_backward(incoming, normed_value, inverse, gain):
        scaled = incoming * gain
        centred = scaled - mean(scaled) - normed_value * mean(scaled * normed_value)
        return centred * inverse

    wait_for(0)
    branch = dot(attended_ref[...], weight_out[...]) + bias_out
    normed_one, inverse_one = normed(x_ref[...].astype(f32) + branch)
    hidden = normed_one * gain_one + shift_one
    hidden_low = hidden.astype(bf16)
    hidden_ref[...] = hidden_low
    mlp_out = jnp.zeros_like(hidden)
    wait_for(1)
    wait_for(2)
    for chunk in range(chunks):
        cols = slice(chunk * width, (chunk + 1) * width)
        upper = dot(hidden_low, weight_up[:, cols]) + bias_up_ref[:, cols]
        share = 0.5 * (1.0 + lax.erf(upper * 0.5**0.5))
        density = jnp.exp(-0.5 * upper * upper) * (2.0 * jnp.pi) ** -0.5
        active = (upper * share).astype(bf16)
        active_ref[:, cols] = active
        slope[:, cols] = share + upper * density
        mlp_out = mlp_out + dot(active, weight_down[cols, :])
    normed_two, inverse_two = normed(hidden + (mlp_out + bias_down))
    out_ref[...] = (normed_two * gain_two + shift_two).astype(bf16)

    incoming = cot_ref[...].astype(f32)
    grad_sum = norm_backward(incoming, normed_two, inverse_two, gain_two)
    grad_mlp = grad_sum.astype(bf16)
    grad_mlp_ref[...] = grad_mlp
    add_to(5, incoming)
    add_to(4, incoming * normed_two)
    add_to(3, grad_mlp)
    grad_hidden = grad_sum
    for chunk in range(chunks):
        cols = slice(chunk * width, (chunk + 1) * width)
        grad_active = dot(grad_mlp, weight_down[cols, :], rows_by_rows)
        grad_upper = (grad_active * slope[:, cols]).astype(bf16)
        grad_upper_ref[:, cols] = grad_upper
        sums_up_ref[0:1, cols] += jnp.sum(grad_upper.astype(f32), axis=0, keepdims=True)
        grad_hidden = grad_hidden + dot(grad_upper, weight_up[:, cols], rows_by_rows)
    grad_pre = norm_backward(grad_hidden, normed_one, inverse_one, gain_one)
    grad_pre_ref[...] = grad_pre
    grad_branch = grad_pre.astype(bf16)
    grad_branch_ref[...] = grad_branch
    add_to(2, grad_hidden)
    add_to(1, grad_hidden * normed_one)
    add_to(0, grad_branch)
    grad_attended_ref[...] = dot(grad_branch, weight_out[...], rows_by_rows).astype(bf16)


def token_parts(attended, x, cotangent, weights, vecs, bias_up):
    tokens, width = x.shape
    shards, part, cols = weights.shape
    hidden_n = (cols - width) // 2
    tile = 256

    def row(n):
        return pl.BlockSpec((tile, n), lambda i: (i, 0))

    def fixed(shape):
        return pl.BlockSpec(shape, lambda i: (0, 0))

    def shape(n, kind=bf16):
        return jax.ShapeDtypeStruct((tokens, n), kind)

    copies = shards * (2 + hidden_n // width)
    return pl.pallas_call(
        token_kernel,
        grid=(tokens // tile,),
        in_specs=[row(width)] * 3
        + [pl.BlockSpec(memory_space=pl.ANY), fixed(vecs.shape), fixed(bias_up.shape)],
        out_specs=[
            row(width),
            row(width),
            row(hidden_n),
            row(width),
            row(hidden_n),
            row(width),
            row(width),
            row(width),
            fixed((8, width)),
            fixed((8, hidden_n)),
        ],
        out_shape=[
            shape(width),
            shape(width),
            shape(hidden_n),
            shape(width),
            shape(hidden_n),
            shape(width, f32),
            shape(width),
            shape(width),
            jax.ShapeDtypeStruct((8, width), f32),
            jax.ShapeDtypeStruct((8, hidden_n), f32),
        ],
        scratch_shapes=[
            pltpu.VMEM((width, width), bf16),
            pltpu.VMEM((width, hidden_n), bf16),
            pltpu.VMEM((hidden_n, width), bf16),
            pltpu.VMEM((tile, hidden_n), f32),
            pltpu.SemaphoreType.DMA((copies,)),
        ],
        compiler_params=pltpu.CompilerParams(vmem_limit_bytes=vmem_cap),
        cost_estimate=pl.CostEstimate(flops=0, bytes_accessed=tokens, transcendentals=0),
        name="token_parts",
    )(attended, x, cotangent, weights, vecs, bias_up)


def body(
    inputs,
    segments,
    random_blocks,
    cotangent,
    qkv_weight,
    qv_bias,
    out_weight,
    out_bias,
    norm1_gain,
    norm1_bias,
    up_weight,
    up_bias,
    down_weight,
    down_bias,
    norm2_gain,
    norm2_bias,
):
    seq_count, run, width = inputs.shape
    per_dev, head_count, rand_count = random_blocks.shape[1:]
    block = run // per_dev
    head_size = width // head_count
    dp_count = lax.axis_size("dp")
    ctx_count = lax.axis_size("ctx")
    ctx_index = lax.axis_index("ctx")
    team = ctx_count // seq_count
    tokens = seq_count * run

    x = swap_pieces(inputs, "ctx", team).reshape(tokens, width)
    lists = swap_pieces(tied(random_blocks.reshape(seq_count, 1, -1), x), "ctx", team)

    def back_to_runs(rows):
        return swap_pieces(rows.reshape(seq_count, run, width), "ctx", team)

    vectors = (qv_bias, out_bias, norm1_gain, norm1_bias, up_bias, down_bias, norm2_gain, norm2_bias)
    sizes = [v.shape[0] for v in vectors]
    qkv_rows, qkv_cols = qkv_weight.shape
    first = lax.all_gather(pack_weights(qkv_weight, vectors), "dp", axis=0)
    others = lax.all_gather(join_weights(out_weight, up_weight, down_weight), "dp", axis=0)

    def vector(place):
        return first[:, qkv_rows + place, : sizes[place]].reshape(1, -1).astype(f32)

    bias_qv, bias_up = vector(0), vector(4)
    vecs = first[:, qkv_rows + 1 : qkv_rows + 8, :qkv_rows].transpose(1, 0, 2).reshape(7, width)
    vecs = jnp.concatenate([vecs[:3], vecs[4:], jnp.zeros_like(vecs[:2])], axis=0).astype(f32)

    seq_index = ctx_index // team
    seg = lax.dynamic_index_in_dim(segments, seq_index, 0, keepdims=False)
    lists = lists.reshape(seq_count, per_dev, head_count, rand_count)
    if team > 1:
        team_index = ctx_index % team
        held = -(-head_count // (2 * team)) * 2
        spare = held * team - head_count
        lists = share_pieces(lists, "ctx", team).transpose(1, 0, 2, 3, 4)
        lists = jnp.pad(lists.reshape(-1, head_count, rand_count), ((0, 0), (0, spare), (0, 0)))
        lists = lax.dynamic_slice_in_dim(lists, team_index * held, held, 1)
    else:
        lists = lists.reshape(-1, head_count, rand_count)
    features = mask_features(seg, lists, block)

    def to_heads(rows):
        if team == 1:
            return rows
        rows = jnp.pad(rows, ((0, 0), (0, spare * head_size)))
        part = swap_pieces(rows.reshape(tokens, team, -1).transpose(1, 0, 2), "ctx", 1)
        part = part.reshape(team, seq_count, run, -1).transpose(1, 0, 2, 3)
        return part.reshape(team * tokens, -1)

    def to_tokens(part):
        if team == 1:
            return part
        part = part.reshape(seq_count, team, run, -1).transpose(1, 0, 2, 3)
        rows = swap_pieces(part.reshape(team, tokens, -1), "ctx", 1)
        return rows.transpose(1, 0, 2).reshape(tokens, -1)[:, :width]

    queries, keys, values = project(x, first, bias_qv)
    grad_result = swap_pieces(copied(cotangent, x), "ctx", team).reshape(tokens, width)
    heads = tuple(to_heads(part) for part in (queries, keys, values))
    attended = attend(forward_kernel, heads, features, 1, head_size, "attend_forward")[0]
    attended = to_tokens(attended)
    parts = token_parts(attended, x, grad_result, others, vecs, bias_up)
    result, hidden_low, active, grad_mlp, grad_upper, grad_pre, grad_branch, grad_att, sums, sums_up = parts

    down_grad = matrix_grad(active, grad_mlp)
    down_part = scattered(down_grad)
    place = lax.axis_index("dp").reshape(1).astype(jnp.int32)
    up = Scatter(*wide_grad(place, hidden_low, grad_upper, dp_count, (down_grad,)))
    sent = up.begin()
    layer_out = back_to_runs(tied(result, sent))
    up.end()
    sent = up.begin(sent)
    back_heads = heads + (to_heads(grad_att),)
    pair_count = back_heads[0].shape[1] // lanes_n
    back = attend(backward_kernel, back_heads, features, 3, head_size, "attend_backward", (sent,))
    if team > 1:
        back = [to_tokens(array) for array in back[:3]]
        back.append(jnp.stack([jnp.sum(back[i].astype(f32), axis=0) for i in (0, 2)]))
    *back, bias_sums = back
    def shard_rows(values):
        return values.reshape(dp_count, -1, qkv_rows).transpose(1, 0, 2).reshape(-1, width)

    side = [shard_rows(bias_sums[:2].reshape(-1)), sums[:6], shard_rows(sums_up[0])]
    side_rows = [part.shape[0] for part in side]
    side_n = -(-sum(side_rows) // lanes_n) * lanes_n
    side.append(jnp.zeros((side_n - sum(side_rows), width), f32))
    wide = Chain([[down_part], up.end(back[0])])
    sent = wide.begin(back[0])
    groups = [(attended, [grad_branch]), (x, back)]
    grads = weight_grads(
        place, groups, jnp.concatenate(side, axis=0), dp_count, (sent, layer_out)
    )
    rest = Scatter(*grads)
    sent = rest.begin()
    result = input_gradient(first, grad_pre, back, (sent,))
    input_grad = back_to_runs(tied(result, sent))
    rest.end(result)
    sent = rest.begin()
    sent = wide.next(sent)
    rest_bits = (ctx_count - 1).bit_length()
    rest = Chain([rest.end(sent)])
    sent = rest.begin(sent)
    while len(wide.plan) > rest_bits + 1:
        sent = wide.next(sent)
    layer_out = copied(layer_out, sent)
    sent = rest.next(sent)
    wide.end(sent)
    pieces = added(wide.parts[0])
    rest.next(pieces, input_grad)
    pieces = lax.all_gather(pieces, "ctx", axis=0)
    while len(rest.plan) > 1:
        sent = rest.next()
    input_grad = copied(input_grad, sent)
    rest.end()
    down_total, up_total = spread_gradients(pieces, qkv_rows)
    total = rest.parts[0][0].astype(f32)
    out_total, qkv_total = total[:, :width], total[:, width : width + qkv_cols]
    flat = total[:, width + qkv_cols : width + qkv_cols + sum(side_rows)].T
    starts = [0, 2, 3, 4, 8, 5, 6, 7]
    vec_totals = [
        flat[start : start + size // qkv_rows].reshape(-1) for start, size in zip(starts, sizes)
    ]
    return (
        layer_out,
        input_grad,
        qkv_total,
        vec_totals[0],
        out_total,
        vec_totals[1],
        vec_totals[2],
        vec_totals[3],
        up_total,
        vec_totals[4],
        down_total,
        vec_totals[5],
        vec_totals[6],
        vec_totals[7],
    )


def solution(mesh):
    tokens = P("dp", "ctx", None)
    matrix, vector = P("dp", None), P("dp")
    weights = (matrix, vector, matrix, vector, vector, vector, matrix, vector, matrix, vector, vector, vector)
    return jax.shard_map(
        body,
        mesh=mesh,
        in_specs=(tokens, matrix, P("dp", "ctx", None, None), tokens) + weights,
        out_specs=(tokens, tokens) + weights,
        check_vma=False,
    )
```

```python
import functools
import math

import jax
import jax.numpy as jnp
from jax import lax
from jax.experimental import pallas as pl
from jax.experimental.pallas import tpu as pltpu
from jax.sharding import PartitionSpec as P

f32, bf16 = jnp.float32, jnp.bfloat16
eps_norm = 1e-12
far = 1e30
doc_min = 200
lanes_n = 128
vmem_cap = 56 * 2**20


def swap_pieces(pieces, axis, stride):
    count, size = pieces.shape[0], lax.axis_size(axis)
    groups = None
    if count < size:
        span = stride * count
        starts = [base + offset for base in range(0, size, span) for offset in range(stride)]
        groups = [[start + i * stride for i in range(count)] for start in starts]
    return lax.all_to_all(pieces, axis, 0, 0, axis_index_groups=groups, tiled=True)


def share_pieces(piece, axis, count):
    size = lax.axis_size(axis)
    member = lax.axis_index(axis) % count
    came, stride = piece[None], 1
    while stride < count:
        other = lax.ppermute(came, axis, [(i, i ^ stride) for i in range(size)])
        upper = (member // stride) % 2 == 1
        came = jnp.concatenate([jnp.where(upper, other, came), jnp.where(upper, came, other)], axis=0)
        stride *= 2
    return came


def tied(value, *deps):
    def nothing(*refs):
        pass

    return pl.pallas_call(
        nothing,
        in_specs=[pl.BlockSpec(memory_space=pl.ANY)] * (1 + len(deps)),
        out_specs=pl.BlockSpec(memory_space=pl.ANY),
        out_shape=jax.ShapeDtypeStruct(value.shape, value.dtype),
        input_output_aliases={0: 0},
        name="tied",
    )(value, *deps)


def added(terms):
    if len(terms) == 1:
        return terms[0]
    total = terms[0].astype(f32)
    for term in terms[1:]:
        total = total + term.astype(f32)
    return total.astype(bf16)


class Chain:
    def __init__(self, parts, axis="ctx"):
        self.parts = parts
        strides, stride = [], 1
        while stride < lax.axis_size(axis):
            strides.append(stride)
            stride *= 2
        self.axis = axis
        self.plan = [(stride, True) for stride in strides]
        if axis == "ctx":
            self.plan += [(stride, False) for stride in reversed(strides)]

    def halves(self, stride):
        member = (lax.axis_index(self.axis) // stride) % 2

        def half(which):
            columns = []
            for terms in self.parts:
                rows = terms[0].shape[0] // 2
                cut = [lax.dynamic_slice_in_dim(term, which * rows, rows, 0) for term in terms]
                columns.append(added(cut))
            return columns[0] if len(columns) == 1 else jnp.concatenate(columns, axis=1)

        return half(member), half(1 - member)

    def begin(self, *after):
        stride, adds = self.plan[0]
        if adds:
            self.kept, sent = self.halves(stride)
            sent = tied(sent, *after)
        else:
            sent = tied(added(self.parts[0]), *after)
            self.kept = sent
        size = lax.axis_size(self.axis)
        self.came = lax.ppermute(sent, self.axis, [(i, i ^ stride) for i in range(size)])
        return sent

    def end(self, *after):
        stride, adds = self.plan.pop(0)
        came = tied(self.came, *after) if after else self.came
        if adds:
            self.parts = [[self.kept, came]]
        else:
            upper = (lax.axis_index(self.axis) // stride) % 2 == 1
            pair = [jnp.where(upper, came, self.kept), jnp.where(upper, self.kept, came)]
            self.parts = [[jnp.concatenate(pair, axis=0)]]
        return self.parts[0]

    def next(self, *after):
        self.end()
        return self.begin(*after)

    def open(self):
        return len(self.plan) > 0


class Scatter:
    def __init__(self, kept, sent):
        self.kept, self.came, self.stride = kept, None, 1
        self.sent = sent

    def begin(self, *after):
        size = lax.axis_size("dp")
        sent = tied(self.sent, *after)
        self.came = lax.ppermute(sent, "dp", [(i, i ^ self.stride) for i in range(size)])
        return sent

    def end(self, *after):
        came = tied(self.came, *after) if after else self.came
        self.stride *= 2
        if self.stride == lax.axis_size("dp"):
            return [self.kept, came]
        rows = self.kept.shape[0] // 2
        self.sent = added([self.kept[rows:], came[rows:]])
        self.kept = added([self.kept[:rows], came[:rows]])
        return None


def copied(value, *deps):
    def copy(value_ref, *refs):
        refs[-1][...] = value_ref[...]

    return pl.pallas_call(
        copy,
        in_specs=[pl.BlockSpec(memory_space=pltpu.VMEM)]
        + [pl.BlockSpec(memory_space=pl.ANY)] * len(deps),
        out_shape=jax.ShapeDtypeStruct(value.shape, value.dtype),
        name="copied",
    )(value, *deps)


def scattered(grad):
    return lax.psum_scatter(grad, "dp", scatter_dimension=0, tiled=True)


def mask_features(seg, rand, block):
    tokens = seg.shape[0]
    blocks, heads = rand.shape[:2]
    seg_limit = tokens // doc_min + 1
    used = seg_limit + 2 * blocks
    width = -(-used // lanes_n) * lanes_n
    ids = jnp.arange(blocks, dtype=jnp.int32)

    def hot(values):
        return (values[..., None] == ids).astype(jnp.int32)

    near = hot(ids - 1) + hot(ids) + hot(ids + 1) + hot(ids * 0) + hot(ids * 0 + blocks - 1)
    counts = near[:, None, :] + jnp.sum(hot(rand), axis=2)
    edge = (ids == 0) | (ids == blocks - 1)
    counts = jnp.where(edge[:, None, None], 1, counts).transpose(1, 2, 0)
    log_count = jnp.log(jnp.maximum(counts, 1).astype(f32))
    high = log_count.astype(bf16).astype(f32)
    low = jnp.where(counts > 0, log_count - high, 0.0)
    high = jnp.where(counts > 0, high, -far)
    table = jnp.concatenate(
        [
            jnp.zeros((heads, blocks, seg_limit), f32),
            high,
            low,
            jnp.zeros((heads, blocks, width - used), f32),
        ],
        axis=2,
    )
    lane = jnp.arange(width, dtype=jnp.int32)[None]
    own = (jnp.arange(tokens, dtype=jnp.int32) // block)[:, None]
    is_seg = lane < seg_limit
    same = lane == seg[:, None]
    key_feat = jnp.where(is_seg & same, 1.0, 0.0).astype(bf16)
    own_lane = (lane - seg_limit == own) | (lane - seg_limit - blocks == own)
    query_feat = jnp.where(
        is_seg, jnp.where(same, 0.0, -far), jnp.where(own_lane, 1.0, 0.0)
    ).astype(bf16)
    near = -(-seg_limit // lanes_n) * lanes_n
    return key_feat[:, :near], query_feat[:, :near], table


def fill_keys(k_ref, key_feat_ref, table_ref, keys):
    tokens, near = key_feat_ref.shape
    blocks, width = table_ref.shape[1:]
    feat = key_feat_ref[...].astype(f32).reshape(blocks, tokens // blocks, near)
    for side in range(2):
        rows = table_ref[side][:, None, :]
        both = (feat + rows[..., :near]).reshape(tokens, near)
        keys[side, :, :lanes_n] = k_ref[...]
        keys[side, :, lanes_n : lanes_n + near] = both.astype(bf16)
        if width > near:
            rest = jnp.broadcast_to(rows[..., near:], (blocks, tokens // blocks, width - near))
            keys[side, :, lanes_n + near :] = rest.reshape(tokens, width - near).astype(bf16)


def query_lanes(near_feat, start, tokens, blocks, width):
    rows, near = near_feat.shape
    if width == near:
        return near_feat
    shape = (rows, width - near)
    lane = lax.broadcasted_iota(jnp.int32, shape, 1) + near - (tokens // doc_min + 1)
    own = (lax.broadcasted_iota(jnp.int32, shape, 0) + start) // (tokens // blocks)
    rest = jnp.where((lane == own) | (lane - blocks == own), 1.0, 0.0).astype(bf16)
    return jnp.concatenate([near_feat, rest], axis=1)


rows_by_rows = (((1,), (1,)), ((), ()))
cols_by_cols = (((0,), (0,)), ((), ()))


def dot(left, right, dims=(((1,), (0,)), ((), ()))):
    return lax.dot_general(left, right, dims, preferred_element_type=f32)


def forward_kernel(
    q_ref,
    k_ref,
    v_ref,
    key_feat_ref,
    query_feat_ref,
    table_ref,
    out_ref,
    log_ref,
    keys,
    vals,
    *,
    half,
    tile,
):
    tokens = q_ref.shape[0]
    fill_keys(k_ref, key_feat_ref, table_ref, keys)
    vals[:, :lanes_n] = v_ref[...]
    vals[:, lanes_n:] = jnp.ones((tokens, lanes_n), bf16)

    @pl.loop(0, tokens // tile)
    def _(step):
        rows = pl.ds(pl.multiple_of(step * tile, tile), tile)
        q = q_ref[rows, :] * bf16(half**-0.5)
        side_of = lax.broadcasted_iota(jnp.int32, (tile, lanes_n), 1) // half
        feat = query_lanes(query_feat_ref[rows, :], step * tile, tokens, *table_ref.shape[1:])
        scores = [
            dot(
                jnp.concatenate([jnp.where(side_of == side, q, bf16(0)), feat], axis=1),
                keys[side],
                rows_by_rows,
            )
            for side in range(2)
        ]
        outs, logs = [], []
        for score in scores:
            top = jnp.max(score, axis=1, keepdims=True)
            weights = jnp.exp(score - top).astype(bf16)
            mixed = dot(weights, vals[...])
            outs.append(mixed[:, :lanes_n] / mixed[:, lanes_n:])
            logs.append(top + jnp.log(mixed[:, lanes_n:]))
        out_ref[rows, :] = jnp.where(side_of == 0, outs[0], outs[1]).astype(bf16)
        log_ref[rows, :] = jnp.where(side_of == 0, logs[0], logs[1])


def backward_kernel(
    q_ref,
    k_ref,
    v_ref,
    grad_ref,
    out_ref,
    log_ref,
    key_feat_ref,
    query_feat_ref,
    table_ref,
    dq_ref,
    dk_ref,
    dv_ref,
    sums_ref,
    keys,
    dk_sum,
    dv_sum,
    *,
    half,
    tile,
):
    tokens = q_ref.shape[0]
    fill_keys(k_ref, key_feat_ref, table_ref, keys)
    dk_sum[...] = jnp.zeros_like(dk_sum)
    dv_sum[...] = jnp.zeros_like(dv_sum)
    sums_ref[...] = jnp.zeros_like(sums_ref)

    @pl.loop(0, tokens // tile)
    def _(step):
        rows = pl.ds(pl.multiple_of(step * tile, tile), tile)
        q_pair = q_ref[rows, :] * bf16(half**-0.5)
        grad_pair = grad_ref[rows, :]
        side_of = lax.broadcasted_iota(jnp.int32, (tile, lanes_n), 1) // half
        feat = query_lanes(query_feat_ref[rows, :], step * tile, tokens, *table_ref.shape[1:])
        queries = [jnp.where(side_of == side, q_pair, bf16(0)) for side in range(2)]
        grads = [jnp.where(side_of == side, grad_pair, bf16(0)) for side in range(2)]
        probs, dscores = [], []
        product = grad_pair.astype(f32) * out_ref[rows, :].astype(f32)
        for side in range(2):
            wide = jnp.concatenate([queries[side], feat], axis=1)
            scores = dot(wide, keys[side], rows_by_rows)
            dprobs = dot(grads[side], v_ref[...], rows_by_rows)
            prob = jnp.exp(scores - log_ref[rows, side * half : side * half + 1])
            inner = jnp.sum(jnp.where(side_of == side, product, 0.0), axis=1, keepdims=True)
            dscore = prob * (dprobs - inner)
            probs.append(prob.astype(bf16))
            dscores.append(dscore.astype(bf16))
        dv_sum[...] += dot(
            jnp.concatenate(probs, axis=0), jnp.concatenate(grads, axis=0), cols_by_cols
        )
        dk_sum[...] += dot(
            jnp.concatenate(dscores, axis=0), jnp.concatenate(queries, axis=0), cols_by_cols
        )
        dqs = [dot(dscore, k_ref[...]) for dscore in dscores]
        dq = (jnp.where(side_of == 0, dqs[0], dqs[1]) * half**-0.5).astype(bf16)
        dq_ref[rows, :] = dq
        sums_ref[0:1, :] += jnp.sum(dq.astype(f32), axis=0, keepdims=True)

    dk_ref[...] = dk_sum[...].astype(bf16)
    dv = dv_sum[...].astype(bf16)
    dv_ref[...] = dv
    sums_ref[1:2, :] = jnp.sum(dv.astype(f32), axis=0, keepdims=True)


def attend(kernel, arrays, features, outs, half, name, after=(), first=0, count=None):
    tokens, width = arrays[0].shape
    key_feat, query_feat, table = features
    count = width // lanes_n if count is None else count
    near, feat_width = key_feat.shape[1], table.shape[2]
    tile = tokens if tokens <= 1024 else 32
    once = {"pipeline_mode": pl.Buffered(1)} if count == 1 else {}
    pair = pl.BlockSpec((tokens, lanes_n), lambda p: (0, p + first), **once)
    pair_out = pl.BlockSpec((tokens, lanes_n), lambda p: (0, p), **once)
    whole = pl.BlockSpec((tokens, near), lambda p: (0, 0), pipeline_mode=pl.Buffered(1))
    shape = jax.ShapeDtypeStruct((tokens, count * lanes_n), bf16)
    scratch = [pltpu.VMEM((2, tokens, lanes_n + feat_width), bf16)]
    if outs == 1:
        scratch = scratch + [pltpu.VMEM((tokens, 2 * lanes_n), bf16)]
    else:
        scratch = scratch + [pltpu.VMEM((tokens, lanes_n), f32)] * 2

    def run(*refs):
        held = len(arrays) + 3
        kernel(*refs[:held], *refs[held + len(after) :], half=half, tile=tile)

    return pl.pallas_call(
        run,
        grid=(count,),
        in_specs=[pair] * len(arrays)
        + [whole, whole]
        + [pl.BlockSpec((2,) + table.shape[1:], lambda p: (p + first, 0, 0))]
        + [pl.BlockSpec(memory_space=pl.ANY)] * len(after),
        out_specs=[pair_out] * outs
        + [pl.BlockSpec((8, lanes_n), lambda p: (0, p)) if outs > 1 else pair_out],
        out_shape=[shape] * outs
        + [jax.ShapeDtypeStruct((8 if outs > 1 else tokens, count * lanes_n), f32)],
        scratch_shapes=scratch,
        compiler_params=pltpu.CompilerParams(vmem_limit_bytes=vmem_cap),
        cost_estimate=pl.CostEstimate(flops=0, bytes_accessed=tokens, transcendentals=0),
        name=name,
    )(*arrays, key_feat, query_feat, table, *after)


def pack_kernel(weight_ref, *refs):
    out_ref = refs[-1]
    rows = weight_ref.shape[0]
    out_ref[:rows, :] = weight_ref[...]
    out_ref[rows:, :] = jnp.zeros_like(out_ref[rows:, :])
    for place, ref in enumerate(refs[:-1]):
        out_ref[rows + place : rows + place + 1, : ref.shape[0]] = ref[...].reshape(1, -1)


def pack_weights(weight, vectors):
    rows, cols = weight.shape
    extra = -(-len(vectors) // 16) * 16
    return pl.pallas_call(
        pack_kernel,
        out_shape=jax.ShapeDtypeStruct((rows + extra, cols), weight.dtype),
        name="pack_weights",
    )(weight, *vectors)


def join_kernel(out_ref, up_ref, down_ref, all_ref):
    rows, width = out_ref.shape
    hidden_n = up_ref.shape[1]
    all_ref[:, :width] = out_ref[...]
    all_ref[:, width : width + hidden_n] = up_ref[...]
    for part in range(hidden_n // width):
        start = width + hidden_n + part * width
        all_ref[:, start : start + width] = down_ref[part * rows : (part + 1) * rows, :]


def join_weights(out_weight, up_weight, down_weight):
    rows, width = out_weight.shape
    return pl.pallas_call(
        join_kernel,
        out_shape=jax.ShapeDtypeStruct((rows, width + 2 * up_weight.shape[1]), out_weight.dtype),
        compiler_params=pltpu.CompilerParams(vmem_limit_bytes=vmem_cap),
        name="join_weights",
    )(out_weight, up_weight, down_weight)


def project_kernel(x_ref, weight_ref, bias_ref, q_ref, k_ref, v_ref, weight, *, part):
    shards = weight_ref.shape[0]
    width = x_ref.shape[1]

    @pl.when(pl.program_id(0) == 0)
    def _():
        for shard in range(shards):
            weight[shard * part : (shard + 1) * part, :] = weight_ref[shard, :part, :]

    x = x_ref[...]
    q_ref[...] = (dot(x, weight[:, :width]) + bias_ref[:, :width]).astype(bf16)
    k_ref[...] = dot(x, weight[:, width : 2 * width]).astype(bf16)
    v_ref[...] = (dot(x, weight[:, 2 * width :]) + bias_ref[:, width:]).astype(bf16)


def project(x, weight, bias):
    tokens, width = x.shape
    tile = min(512, tokens)
    row = pl.BlockSpec((tile, width), lambda i: (i, 0))
    shape = jax.ShapeDtypeStruct((tokens, width), bf16)
    return pl.pallas_call(
        functools.partial(project_kernel, part=width // weight.shape[0]),
        grid=(tokens // tile,),
        in_specs=[
            row,
            pl.BlockSpec(weight.shape, lambda i: (0, 0, 0), pipeline_mode=pl.Buffered(1)),
            pl.BlockSpec(bias.shape, lambda i: (0, 0)),
        ],
        out_specs=[row] * 3,
        out_shape=[shape] * 3,
        scratch_shapes=[pltpu.VMEM((width, weight.shape[2]), bf16)],
        compiler_params=pltpu.CompilerParams(vmem_limit_bytes=vmem_cap),
        cost_estimate=pl.CostEstimate(flops=0, bytes_accessed=tokens, transcendentals=0),
        name="project",
    )(x, weight, bias)


def sort_shards(place_ref, grad, kept_ref, sent_ref, shards, block, block_n):
    rows = grad.shape[0] // shards
    for shard in range(shards):
        turn = place_ref[0] ^ shard
        start = pl.multiple_of(((turn // 2) * block_n + block) * rows, rows)
        piece = grad[shard * rows : (shard + 1) * rows].astype(bf16)

        @pl.when(turn % 2 == 0)
        def _():
            kept_ref[pl.ds(start, rows), : grad.shape[1]] = piece

        @pl.when(turn % 2 == 1)
        def _():
            sent_ref[pl.ds(start, rows), : grad.shape[1]] = piece


def grads_kernel(place_ref, *refs, groups, held, shards):
    kept_ref, sent_ref = refs[-2:]
    grads = []
    for left, rights in groups:
        right = [refs[place][...] for place in rights]
        right = right[0] if len(right) == 1 else jnp.concatenate(right, axis=1)
        grads.append(dot(refs[left][...], right, cols_by_cols).astype(bf16))
    grads.append(jnp.transpose(refs[held - 1][...]).astype(bf16))
    sort_shards(place_ref, jnp.concatenate(grads, axis=1), kept_ref, sent_ref, shards, 0, 1)


def weight_grads(place, groups, extra, shards, after=()):
    arrays, places = [], []
    for left, rights in groups:
        places.append((len(arrays), tuple(range(len(arrays) + 1, len(arrays) + 1 + len(rights)))))
        arrays += [left] + list(rights)
    arrays.append(extra)
    cols = sum(right.shape[1] for _, rights in groups for right in rights) + extra.shape[0]
    held = len(arrays)
    half = jax.ShapeDtypeStruct((groups[0][0].shape[1] // 2, cols), bf16)
    return pl.pallas_call(
        functools.partial(grads_kernel, groups=places, held=held, shards=shards),
        in_specs=[pl.BlockSpec(memory_space=pltpu.SMEM)]
        + [pl.BlockSpec(memory_space=pltpu.VMEM)] * held
        + [pl.BlockSpec(memory_space=pl.ANY)] * len(after),
        out_shape=[half] * 2,
        compiler_params=pltpu.CompilerParams(vmem_limit_bytes=vmem_cap),
        cost_estimate=pl.CostEstimate(flops=0, bytes_accessed=cols, transcendentals=0),
        name="weight_grads",
    )(place, *arrays, *after)


def wide_grad_kernel(place_ref, left_ref, right_ref, *refs, shards):
    grad = dot(left_ref[...], right_ref[...], cols_by_cols)
    sort_shards(
        place_ref, grad, refs[-2], refs[-1], shards, pl.program_id(0), pl.num_programs(0)
    )


def wide_grad(place, left, right, shards, after=()):
    tokens, rows = left.shape
    runs = right.shape[1] // rows
    half = (rows * runs // 2, rows)
    whole = pl.BlockSpec(half, lambda i: (0, 0))
    return pl.pallas_call(
        functools.partial(wide_grad_kernel, shards=shards),
        grid=(runs,),
        in_specs=[
            pl.BlockSpec(memory_space=pltpu.SMEM),
            pl.BlockSpec((tokens, rows), lambda i: (0, 0)),
            pl.BlockSpec((tokens, rows), lambda i: (0, i)),
        ]
        + [pl.BlockSpec(memory_space=pl.ANY)] * len(after),
        out_specs=[whole] * 2,
        out_shape=[jax.ShapeDtypeStruct(half, bf16)] * 2,
        compiler_params=pltpu.CompilerParams(vmem_limit_bytes=vmem_cap),
        cost_estimate=pl.CostEstimate(flops=0, bytes_accessed=rows, transcendentals=0),
        name="wide_grad",
    )(place, left, right, *after)


def matrix_grad_kernel(left_ref, right_ref, *refs):
    refs[-1][...] = dot(left_ref[...], right_ref[...], cols_by_cols).astype(bf16)


def matrix_grad(left, right, after=()):
    tokens, rows = left.shape
    cols = right.shape[1]
    run = min(rows, cols)
    tall = rows > cols

    def taken(yes):
        return pl.BlockSpec((tokens, run), (lambda i: (0, i)) if yes else (lambda i: (0, 0)))

    return pl.pallas_call(
        matrix_grad_kernel,
        grid=(max(rows, cols) // run,),
        in_specs=[taken(tall), taken(not tall)] + [pl.BlockSpec(memory_space=pl.ANY)] * len(after),
        out_specs=pl.BlockSpec((run, run), (lambda i: (i, 0)) if tall else (lambda i: (0, i))),
        out_shape=jax.ShapeDtypeStruct((rows, cols), bf16),
        compiler_params=pltpu.CompilerParams(vmem_limit_bytes=vmem_cap),
        cost_estimate=pl.CostEstimate(flops=0, bytes_accessed=cols, transcendentals=0),
        name="matrix_grad",
    )(left, right, *after)


def spread_kernel(pieces_ref, down_ref, up_ref):
    count, rows, cols = pieces_ref.shape
    width = cols // 2
    part = up_ref.shape[0]
    bits = (count - 1).bit_length()
    for device in range(count):
        place = sum(((device >> bit) & 1) << (bits - 1 - bit) for bit in range(bits))
        piece = pieces_ref[device].astype(f32)
        down_ref[place * rows : (place + 1) * rows, :] = piece[:, :width]
        for start in range(0, rows, math.gcd(rows, part)):
            size = math.gcd(rows, part)
            run, row = divmod(place * rows + start, part)
            cells = piece[start : start + size, width:]
            up_ref[row : row + size, run * width : (run + 1) * width] = cells


def spread_gradients(pieces, part):
    count, rows, cols = pieces.shape
    width = cols // 2
    return pl.pallas_call(
        spread_kernel,
        out_shape=[
            jax.ShapeDtypeStruct((count * rows, width), f32),
            jax.ShapeDtypeStruct((part, count * rows // part * width), f32),
        ],
        compiler_params=pltpu.CompilerParams(vmem_limit_bytes=vmem_cap),
        name="spread_gradients",
    )(pieces)


def input_kernel(*refs, part, parts_n):
    weight_ref, pre_ref = refs[0], refs[1]
    out_ref, weight = refs[-2], refs[-1]
    shards = weight_ref.shape[0]

    @pl.when(pl.program_id(0) == 0)
    def _():
        for shard in range(shards):
            weight[shard * part : (shard + 1) * part, :] = weight_ref[shard, :part, :]

    grads = jnp.concatenate([ref[...] for ref in refs[2 : 2 + parts_n]], axis=1)
    out_ref[...] = (pre_ref[...] + dot(grads, weight[...], rows_by_rows)).astype(bf16)


def input_gradient(weight, grad_pre, parts, after):
    tokens, width = grad_pre.shape
    tile = min(512, tokens)

    def row(n):
        return pl.BlockSpec((tile, n), lambda i: (i, 0))

    return pl.pallas_call(
        functools.partial(input_kernel, part=width // weight.shape[0], parts_n=len(parts)),
        grid=(tokens // tile,),
        in_specs=[pl.BlockSpec(weight.shape, lambda i: (0, 0, 0), pipeline_mode=pl.Buffered(1))]
        + [row(width)]
        + [row(part.shape[1]) for part in parts]
        + [pl.BlockSpec(memory_space=pl.ANY)] * len(after),
        out_specs=row(width),
        out_shape=jax.ShapeDtypeStruct((tokens, width), bf16),
        scratch_shapes=[pltpu.VMEM((width, weight.shape[2]), bf16)],
        compiler_params=pltpu.CompilerParams(vmem_limit_bytes=vmem_cap),
        cost_estimate=pl.CostEstimate(flops=0, bytes_accessed=tokens, transcendentals=0),
        name="input_gradient",
    )(weight, grad_pre, *parts, *after)


def token_kernel(
    attended_ref,
    x_ref,
    cot_ref,
    weights_ref,
    vec_ref,
    bias_up_ref,
    out_ref,
    hidden_ref,
    active_ref,
    grad_mlp_ref,
    grad_upper_ref,
    grad_pre_ref,
    grad_branch_ref,
    grad_attended_ref,
    sums_ref,
    sums_up_ref,
    weight_out,
    weight_up,
    weight_down,
    slope,
    arrived,
):
    shards, part = weights_ref.shape[:2]
    width, hidden_n = weight_up.shape
    chunks = hidden_n // width

    copies = [[], [], []]
    for shard in range(shards):
        rows = pl.ds(shard * part, part)
        mine = weights_ref.at[shard]
        copies[0].append((mine.at[:, pl.ds(0, width)], weight_out.at[rows, :]))
        copies[1].append((mine.at[:, pl.ds(width, hidden_n)], weight_up.at[rows, :]))
        for chunk in range(chunks):
            start = width + hidden_n + chunk * width
            rows = pl.ds((shard * chunks + chunk) * part, part)
            copies[2].append((mine.at[:, pl.ds(start, width)], weight_down.at[rows, :]))
    starts = [0, shards, 2 * shards]
    copies = [
        [
            pltpu.make_async_copy(source, target, arrived.at[start + place])
            for place, (source, target) in enumerate(some)
        ]
        for start, some in zip(starts, copies)
    ]

    def wait_for(place):
        @pl.when(pl.program_id(0) == 0)
        def _():
            for copy in copies[place]:
                copy.wait()

    @pl.when(pl.program_id(0) == 0)
    def _():
        for some in copies:
            for copy in some:
                copy.start()
        sums_ref[...] = jnp.zeros_like(sums_ref)
        sums_up_ref[...] = jnp.zeros_like(sums_up_ref)

    bias_out, gain_one, shift_one, bias_down, gain_two, shift_two = [
        vec_ref[place : place + 1, :] for place in range(6)
    ]

    def mean(value):
        return jnp.mean(value, axis=1, keepdims=True)

    def add_to(place, value):
        sums_ref[place : place + 1, :] += jnp.sum(value.astype(f32), axis=0, keepdims=True)

    def normed(value):
        centred = value - mean(value)
        inverse = lax.rsqrt(mean(centred * centred) + eps_norm)
        return centred * inverse, inverse

    def norm_backward(incoming, normed_value, inverse, gain):
        scaled = incoming * gain
        centred = scaled - mean(scaled) - normed_value * mean(scaled * normed_value)
        return centred * inverse

    wait_for(0)
    branch = dot(attended_ref[...], weight_out[...]) + bias_out
    normed_one, inverse_one = normed(x_ref[...].astype(f32) + branch)
    hidden = normed_one * gain_one + shift_one
    hidden_low = hidden.astype(bf16)
    hidden_ref[...] = hidden_low
    mlp_out = jnp.zeros_like(hidden)
    wait_for(1)
    wait_for(2)
    for chunk in range(chunks):
        cols = slice(chunk * width, (chunk + 1) * width)
        upper = dot(hidden_low, weight_up[:, cols]) + bias_up_ref[:, cols]
        share = 0.5 * (1.0 + lax.erf(upper * 0.5**0.5))
        density = jnp.exp(-0.5 * upper * upper) * (2.0 * jnp.pi) ** -0.5
        active = (upper * share).astype(bf16)
        active_ref[:, cols] = active
        slope[:, cols] = share + upper * density
        mlp_out = mlp_out + dot(active, weight_down[cols, :])
    normed_two, inverse_two = normed(hidden + (mlp_out + bias_down))
    out_ref[...] = (normed_two * gain_two + shift_two).astype(bf16)

    incoming = cot_ref[...].astype(f32)
    grad_sum = norm_backward(incoming, normed_two, inverse_two, gain_two)
    grad_mlp = grad_sum.astype(bf16)
    grad_mlp_ref[...] = grad_mlp
    add_to(5, incoming)
    add_to(4, incoming * normed_two)
    add_to(3, grad_mlp)
    grad_hidden = grad_sum
    for chunk in range(chunks):
        cols = slice(chunk * width, (chunk + 1) * width)
        grad_active = dot(grad_mlp, weight_down[cols, :], rows_by_rows)
        grad_upper = (grad_active * slope[:, cols]).astype(bf16)
        grad_upper_ref[:, cols] = grad_upper
        sums_up_ref[0:1, cols] += jnp.sum(grad_upper.astype(f32), axis=0, keepdims=True)
        grad_hidden = grad_hidden + dot(grad_upper, weight_up[:, cols], rows_by_rows)
    grad_pre = norm_backward(grad_hidden, normed_one, inverse_one, gain_one)
    grad_pre_ref[...] = grad_pre
    grad_branch = grad_pre.astype(bf16)
    grad_branch_ref[...] = grad_branch
    add_to(2, grad_hidden)
    add_to(1, grad_hidden * normed_one)
    add_to(0, grad_branch)
    grad_attended_ref[...] = dot(grad_branch, weight_out[...], rows_by_rows).astype(bf16)


def token_parts(attended, x, cotangent, weights, vecs, bias_up):
    tokens, width = x.shape
    shards, part, cols = weights.shape
    hidden_n = (cols - width) // 2
    tile = 256

    def row(n):
        return pl.BlockSpec((tile, n), lambda i: (i, 0))

    def fixed(shape):
        return pl.BlockSpec(shape, lambda i: (0, 0))

    def shape(n, kind=bf16):
        return jax.ShapeDtypeStruct((tokens, n), kind)

    copies = shards * (2 + hidden_n // width)
    return pl.pallas_call(
        token_kernel,
        grid=(tokens // tile,),
        in_specs=[row(width)] * 3
        + [pl.BlockSpec(memory_space=pl.ANY), fixed(vecs.shape), fixed(bias_up.shape)],
        out_specs=[
            row(width),
            row(width),
            row(hidden_n),
            row(width),
            row(hidden_n),
            row(width),
            row(width),
            row(width),
            fixed((8, width)),
            fixed((8, hidden_n)),
        ],
        out_shape=[
            shape(width),
            shape(width),
            shape(hidden_n),
            shape(width),
            shape(hidden_n),
            shape(width, f32),
            shape(width),
            shape(width),
            jax.ShapeDtypeStruct((8, width), f32),
            jax.ShapeDtypeStruct((8, hidden_n), f32),
        ],
        scratch_shapes=[
            pltpu.VMEM((width, width), bf16),
            pltpu.VMEM((width, hidden_n), bf16),
            pltpu.VMEM((hidden_n, width), bf16),
            pltpu.VMEM((tile, hidden_n), f32),
            pltpu.SemaphoreType.DMA((copies,)),
        ],
        compiler_params=pltpu.CompilerParams(vmem_limit_bytes=vmem_cap),
        cost_estimate=pl.CostEstimate(flops=0, bytes_accessed=tokens, transcendentals=0),
        name="token_parts",
    )(attended, x, cotangent, weights, vecs, bias_up)


def body(
    inputs,
    segments,
    random_blocks,
    cotangent,
    qkv_weight,
    qv_bias,
    out_weight,
    out_bias,
    norm1_gain,
    norm1_bias,
    up_weight,
    up_bias,
    down_weight,
    down_bias,
    norm2_gain,
    norm2_bias,
):
    seq_count, run, width = inputs.shape
    per_dev, head_count, rand_count = random_blocks.shape[1:]
    block = run // per_dev
    head_size = width // head_count
    dp_count = lax.axis_size("dp")
    ctx_count = lax.axis_size("ctx")
    ctx_index = lax.axis_index("ctx")
    team = ctx_count // seq_count
    tokens = seq_count * run

    x = swap_pieces(inputs, "ctx", team).reshape(tokens, width)
    lists = swap_pieces(tied(random_blocks.reshape(seq_count, 1, -1), x), "ctx", team)

    def back_to_runs(rows):
        return swap_pieces(rows.reshape(seq_count, run, width), "ctx", team)

    vectors = (qv_bias, out_bias, norm1_gain, norm1_bias, up_bias, down_bias, norm2_gain, norm2_bias)
    sizes = [v.shape[0] for v in vectors]
    qkv_rows, qkv_cols = qkv_weight.shape
    first = lax.all_gather(pack_weights(qkv_weight, vectors), "dp", axis=0)
    others = lax.all_gather(join_weights(out_weight, up_weight, down_weight), "dp", axis=0)

    def vector(place):
        return first[:, qkv_rows + place, : sizes[place]].reshape(1, -1).astype(f32)

    bias_qv, bias_up = vector(0), vector(4)
    vecs = first[:, qkv_rows + 1 : qkv_rows + 8, :qkv_rows].transpose(1, 0, 2).reshape(7, width)
    vecs = jnp.concatenate([vecs[:3], vecs[4:], jnp.zeros_like(vecs[:2])], axis=0).astype(f32)

    seq_index = ctx_index // team
    seg = lax.dynamic_index_in_dim(segments, seq_index, 0, keepdims=False)
    lists = lists.reshape(seq_count, per_dev, head_count, rand_count)
    if team > 1:
        team_index = ctx_index % team
        held = -(-head_count // (2 * team)) * 2
        spare = held * team - head_count
        lists = share_pieces(lists, "ctx", team).transpose(1, 0, 2, 3, 4)
        lists = jnp.pad(lists.reshape(-1, head_count, rand_count), ((0, 0), (0, spare), (0, 0)))
        lists = lax.dynamic_slice_in_dim(lists, team_index * held, held, 1)
    else:
        lists = lists.reshape(-1, head_count, rand_count)
    features = mask_features(seg, lists, block)

    def to_heads(rows):
        if team == 1:
            return rows
        rows = jnp.pad(rows, ((0, 0), (0, spare * head_size)))
        part = swap_pieces(rows.reshape(tokens, team, -1).transpose(1, 0, 2), "ctx", 1)
        part = part.reshape(team, seq_count, run, -1).transpose(1, 0, 2, 3)
        return part.reshape(team * tokens, -1)

    def to_tokens(part):
        if team == 1:
            return part
        part = part.reshape(seq_count, team, run, -1).transpose(1, 0, 2, 3)
        rows = swap_pieces(part.reshape(team, tokens, -1), "ctx", 1)
        return rows.transpose(1, 0, 2).reshape(tokens, -1)[:, :width]

    queries, keys, values = project(x, first, bias_qv)
    grad_result = swap_pieces(copied(cotangent, x), "ctx", team).reshape(tokens, width)
    heads = tuple(to_heads(part) for part in (queries, keys, values))
    attended = attend(forward_kernel, heads, features, 1, head_size, "attend_forward")
    attended, log_total = attended
    kept = (attended, log_total)
    attended = to_tokens(attended)
    parts = token_parts(attended, x, grad_result, others, vecs, bias_up)
    result, hidden_low, active, grad_mlp, grad_upper, grad_pre, grad_branch, grad_att, sums, sums_up = parts

    down_grad = matrix_grad(active, grad_mlp)
    down_part = scattered(down_grad)
    place = lax.axis_index("dp").reshape(1).astype(jnp.int32)
    up = Scatter(*wide_grad(place, hidden_low, grad_upper, dp_count, (down_grad,)))
    sent = up.begin()
    layer_out = back_to_runs(tied(result, sent))
    up.end()
    sent = up.begin(sent)
    back_heads = heads + (to_heads(grad_att),) + kept
    pair_count = back_heads[0].shape[1] // lanes_n
    back = attend(backward_kernel, back_heads, features, 3, head_size, "attend_backward", (sent,))
    if team > 1:
        back = [to_tokens(array) for array in back[:3]]
        back.append(jnp.stack([jnp.sum(back[i].astype(f32), axis=0) for i in (0, 2)]))
    *back, bias_sums = back
    def shard_rows(values):
        return values.reshape(dp_count, -1, qkv_rows).transpose(1, 0, 2).reshape(-1, width)

    side = [shard_rows(bias_sums[:2].reshape(-1)), sums[:6], shard_rows(sums_up[0])]
    side_rows = [part.shape[0] for part in side]
    side_n = -(-sum(side_rows) // lanes_n) * lanes_n
    side.append(jnp.zeros((side_n - sum(side_rows), width), f32))
    wide = Chain([[down_part], up.end(back[0])])
    sent = wide.begin(back[0])
    groups = [(attended, [grad_branch]), (x, back)]
    grads = weight_grads(
        place, groups, jnp.concatenate(side, axis=0), dp_count, (sent, layer_out)
    )
    rest = Scatter(*grads)
    sent = rest.begin()
    result = input_gradient(first, grad_pre, back, (sent,))
    input_grad = back_to_runs(tied(result, sent))
    rest.end(result)
    sent = rest.begin()
    sent = wide.next(sent)
    rest_bits = (ctx_count - 1).bit_length()
    rest = Chain([rest.end(sent)])
    sent = rest.begin(sent)
    while len(wide.plan) > rest_bits + 1:
        sent = wide.next(sent)
    layer_out = copied(layer_out, sent)
    sent = rest.next(sent)
    wide.end(sent)
    pieces = added(wide.parts[0])
    rest.next(pieces, input_grad)
    pieces = lax.all_gather(pieces, "ctx", axis=0)
    while len(rest.plan) > 1:
        sent = rest.next()
    input_grad = copied(input_grad, sent)
    rest.end()
    down_total, up_total = spread_gradients(pieces, qkv_rows)
    total = rest.parts[0][0].astype(f32)
    out_total, qkv_total = total[:, :width], total[:, width : width + qkv_cols]
    flat = total[:, width + qkv_cols : width + qkv_cols + sum(side_rows)].T
    starts = [0, 2, 3, 4, 8, 5, 6, 7]
    vec_totals = [
        flat[start : start + size // qkv_rows].reshape(-1) for start, size in zip(starts, sizes)
    ]
    return (
        layer_out,
        input_grad,
        qkv_total,
        vec_totals[0],
        out_total,
        vec_totals[1],
        vec_totals[2],
        vec_totals[3],
        up_total,
        vec_totals[4],
        down_total,
        vec_totals[5],
        vec_totals[6],
        vec_totals[7],
    )


def solution(mesh):
    tokens = P("dp", "ctx", None)
    matrix, vector = P("dp", None), P("dp")
    weights = (matrix, vector, matrix, vector, vector, vector, matrix, vector, matrix, vector, vector, vector)
    return jax.shard_map(
        body,
        mesh=mesh,
        in_specs=(tokens, matrix, P("dp", "ctx", None, None), tokens) + weights,
        out_specs=(tokens, tokens) + weights,
        check_vma=False,
    )
```
